32 devices in a mesh: groups: 2 (over y), tp: 4 (over z), pp: 2 (over x), dp: 2 (over core).
Axes of the slice: x: 2, y: 2, z: 4, core: 2. Of those that a mesh axis runs over, the one named last changes fastest.
Arguments:
- hidden: bfloat16 [4, 4, 64, 5120], P(('groups', 'pp'), None, 'dp', 'tp'), parts along dimension 0, may hold values from -6 to 6
- w_kv: bfloat16 [4, 5120, 2048], P(('groups', 'pp'), 'tp'), parts along dimension 0, may hold values from -0.078125 to 0.078125
- queries: bfloat16 [4, 4, 64, 4096], P(('groups', 'pp'), None, 'dp', 'tp'), parts along dimension 0, may hold values from -8 to 8
- cache: bfloat16 [4, 64, 16, 128, 256], P(('groups', 'pp'), 'dp', 'tp'), parts along dimension 0, may hold values from -4 to 4
- cache_lengths: int32 [128], P(('groups', 'dp')), parts along dimension 0, may hold values from 2 to 256
- updated: int32 [4, 5120], P(('groups', 'pp'), 'tp'), parts along dimension 0, may hold values from 0 to 1, as said below
- delta_values: bfloat16 [32, 8, 8, 128], P(('groups', 'tp', 'pp', 'dp')), parts along dimension 0, may hold values from -4 to 4
- delta_scales: bfloat16 [32, 8, 8], P(('groups', 'tp', 'pp', 'dp')), parts along dimension 0, may hold values from 0.0039978027 to 0.039794922
- delta_targets: int32 [32, 8, 8], P(('groups', 'tp', 'pp', 'dp')), parts along dimension 0, may hold values from 0 to 20479
- send_counts: int32 [32, 8], P(('groups', 'tp', 'pp', 'dp')), parts along dimension 0, may hold values from 0 to 8, as said below
Outputs:
- new_entries: bfloat16 [4, 4, 64, 2048], P(('groups', 'pp'), None, 'dp', 'tp'), parts along dimension 0
- attention_out: bfloat16 [4, 4, 64, 4096], P(('groups', 'pp'), None, 'dp', 'tp'), parts along dimension 0
The draws below stay inside these ranges and needn't reach their ends.
There are 2 independent parts, one for each index of `groups`. The reference program is written for one: setup_inputs(seed, part) draws one part's arguments, and reference() takes and returns one part's arrays. A program takes and returns all parts, laid end to end along the dimension named above; each array names one. Nothing has to cross between parts.
Inputs may be any that keep to these rules, and one draw needn't show every extreme that they name: `send_counts`: at most 8; every sender fills all 8 slots of some owner, and one owner receives 8 live blocks from every sender. `updated`: rows of all but half of the 2 layers, rounded down, are 0.
All inputs are finite; a program needn't handle non-finite values.
Results may differ from the reference program's by a relative error of at most 0.01.
Values may be sent and summed in bfloat16 or wider, within the bound.
A program may use at most 128 MiB of HBM per device.

```python
import math
import jax
import jax.numpy as jnp
from jax import lax

D = 5120
KVH = 8
HD = 128
QH = 32
BLOCK = 128
STEPS = 4
CH = 128
SLOTS = 8
LAYERS = 2
ROWS = 64
SHARD = 1280
KVW = 2048
TARGETS = 20480
OWNERS = 8
SENDERS = 16
N_TP = 4


def draw_queries(key, part):
    key = jax.random.fold_in(key, 11)
    return jnp.clip(jax.random.normal(key, (LAYERS, STEPS, ROWS, QH * HD), jnp.float32), -4.0, 4.0).astype(jnp.bfloat16)


def draw_cache(key, part):
    key = jax.random.fold_in(key, 12)
    return jnp.clip(jax.random.normal(key, (LAYERS, ROWS, 2 * KVH, CH, 2 * HD), jnp.float32), -4.0, 4.0).astype(jnp.bfloat16)


def draw_updated(key, part):
    key = jax.random.fold_in(key, 31)
    layer_key, row_key = jax.random.split(key)
    shuffled = jax.random.permutation(layer_key, LAYERS)
    layer_on = shuffled < LAYERS // 2
    row_on = jax.random.randint(row_key, (LAYERS, D), 0, 4) > 0
    return (layer_on[:, None] & row_on).astype(jnp.int32)


def draw_send_counts(key, part):
    key = jax.random.fold_in(key, 21)
    first_key, second_key, third_key = jax.random.split(key, 3)
    counts = jax.random.randint(first_key, (SENDERS, OWNERS), 0, SLOTS + 1)
    full_owner = jax.random.randint(second_key, (), 0, OWNERS)
    own_full = jax.random.randint(third_key, (SENDERS,), 0, OWNERS)
    owner_index = jnp.arange(OWNERS)[None, :]
    filled = (owner_index == full_owner) | (owner_index == own_full[:, None])
    return jnp.where(filled, SLOTS, counts).astype(jnp.int32)


def plant(drawn, rng, least, largest):
    place = [jax.random.randint(jax.random.fold_in(rng, axis), (), 0, length) for axis, length in enumerate(drawn.shape)]
    longest = drawn.shape.index(max(drawn.shape))
    neighbour = place[:longest] + [(place[longest] + 1) % drawn.shape[longest]] + place[longest + 1:]
    return drawn.at[tuple(place)].set(least).at[tuple(neighbour)].set(largest)


def levels(stream_key, dims, cuts, least, largest):
    def one(axis_at, parts):
        steps = jax.random.uniform(jax.random.fold_in(jax.random.fold_in(stream_key, 6), axis_at), (parts,), jnp.float32, least / len(cuts), largest / len(cuts))
        return jnp.repeat(jnp.exp(steps), dims[axis_at] // parts).reshape((-1,) + (1,) * (len(dims) - axis_at - 1))

    gain = one(*cuts[0])
    for cut in cuts[1:]:
        gain = gain * one(*cut)
    return gain


def scatter_about(rng, dims, scale, bound, cuts=(), kind=jnp.bfloat16):
    drawn = jax.random.normal(rng, dims, jnp.float32) * scale
    if len(cuts) > 0:
        drawn = levels(rng, dims, cuts, -0.22, 0.18) * drawn
    return jnp.clip(drawn, min=-bound, max=bound).astype(kind)


def setup_inputs(seed: int = 0, part: int = 0) -> dict:
    keys = jax.random.split(jax.random.key(seed), 11)
    own_keys = jax.random.split(jax.random.fold_in(keys[10], part), 11)
    hidden = scatter_about(own_keys[0], (LAYERS, STEPS, ROWS, D), 1.0, 6.0, ((0, 2), (2, 2), (3, 4)))
    w_kv = scatter_about(own_keys[1], (LAYERS, D, KVW), D ** -0.5, 0.078125, ((0, 2), (1, 4)))
    queries = draw_queries(jax.random.fold_in(jax.random.fold_in(keys[10], part), 71), part)
    cache = draw_cache(jax.random.fold_in(jax.random.fold_in(keys[10], part), 71), part)
    cache_lengths = plant(jax.random.randint(own_keys[4], (ROWS,), 2, 2 * CH + 1), jax.random.fold_in(own_keys[4], 1), 2, 2 * CH).astype(jnp.int32)
    updated = draw_updated(jax.random.fold_in(jax.random.fold_in(keys[10], part), 71), part)
    delta_values = scatter_about(own_keys[6], (SENDERS, OWNERS, SLOTS, BLOCK), 1.0, 4.0, ((0, 16),))
    delta_scales = jnp.clip(jnp.exp(math.log(0.039794922) - 2.2979944 * jax.random.uniform(own_keys[7], (SENDERS, OWNERS, SLOTS), jnp.float32) ** levels(own_keys[7], (SENDERS, OWNERS, SLOTS), ((0, 16),), -0.2, 0.2)), 0.0039978027, 0.039794922).astype(jnp.bfloat16)
    delta_targets = plant(jax.random.randint(own_keys[8], (SENDERS, OWNERS, SLOTS), 0, TARGETS), jax.random.fold_in(own_keys[8], 1), 0, TARGETS - 1).astype(jnp.int32)
    send_counts = draw_send_counts(jax.random.fold_in(jax.random.fold_in(keys[10], part), 71), part)
    return {"hidden": hidden, "w_kv": w_kv, "queries": queries, "cache": cache, "cache_lengths": cache_lengths, "updated": updated, "delta_values": delta_values, "delta_scales": delta_scales, "delta_targets": delta_targets, "send_counts": send_counts}


ROPE_BASE = 1000000.0
NEG_FILL = -1e+30

def rotate(vectors, positions):
    half_size = vectors.shape[-1] // 2
    index_f = jnp.arange(half_size).astype(jnp.float32)
    inverse = jnp.exp(index_f * (-2.0 / vectors.shape[-1]) * math.log(ROPE_BASE))
    angles = positions[..., None] * inverse
    cosine_table = jnp.cos(angles)
    sine_table = jnp.sin(angles)
    first_half = vectors[..., :half_size]
    second_half = vectors[..., half_size:]
    return jnp.concatenate([first_half * cosine_table - second_half * sine_table, second_half * cosine_table + first_half * sine_table], -1)

def reference(hidden, w_kv, queries, cache, cache_lengths, updated, delta_values, delta_scales, delta_targets, send_counts):
    live_slots = jnp.arange(SLOTS).astype(jnp.int32)[None, None, :] < send_counts[:, :, None]
    factor = jnp.where(live_slots, delta_scales.astype(jnp.float32), jnp.float32(0.0))
    contribution = delta_values.astype(jnp.float32) * factor[..., None]
    owner_index = jnp.broadcast_to(jnp.arange(OWNERS).astype(jnp.int32)[None, :, None], delta_targets.shape)
    dense_delta = jnp.zeros((OWNERS, TARGETS, BLOCK), jnp.float32).at[owner_index, delta_targets].add(contribution)
    dense_delta = dense_delta.reshape(N_TP, LAYERS, SHARD, KVW).transpose(1, 0, 2, 3).reshape(LAYERS, D, KVW)
    merged = (w_kv.astype(jnp.float32) + dense_delta).astype(jnp.bfloat16)
    refreshed = jnp.where(updated[:, :, None] == 1, merged, w_kv)

    def project_layer(layer_pair):
        layer_rows, layer_weight = layer_pair
        row_parts = layer_rows.reshape(STEPS * ROWS, N_TP, SHARD).astype(jnp.float32)
        weight_parts = layer_weight.reshape(N_TP, SHARD, KVW).astype(jnp.float32)
        partial_sums = jnp.einsum('nik,ikc->inc', row_parts, weight_parts, precision=lax.Precision.HIGHEST)
        rounded = lax.optimization_barrier(partial_sums.astype(jnp.bfloat16))
        return lax.optimization_barrier(jnp.sum(rounded.astype(jnp.float32), 0)).reshape(STEPS, ROWS, KVW)
    projected = lax.map(project_layer, (hidden, refreshed))
    step_index = jnp.arange(STEPS).astype(jnp.int32)
    positions = (cache_lengths[None, :] + step_index[:, None]).astype(jnp.float32)
    key_part = projected[..., :KVH * HD].reshape(LAYERS, STEPS, ROWS, KVH, HD)
    new_keys = rotate(key_part, positions[None, :, :, None]).astype(jnp.bfloat16)
    new_values = projected[..., KVH * HD:].astype(jnp.bfloat16).reshape(LAYERS, STEPS, ROWS, KVH, HD)
    new_entries = jnp.concatenate([new_keys.reshape(LAYERS, STEPS, ROWS, KVH * HD), new_values.reshape(LAYERS, STEPS, ROWS, KVH * HD)], -1)
    score_scale = 1.0 / math.sqrt(HD)
    query_rows = queries.reshape(LAYERS, STEPS, ROWS, 2, KVH, 2, HD).transpose(0, 1, 2, 4, 3, 5, 6)
    query_rows = query_rows.reshape(LAYERS, STEPS, ROWS, KVH, 4, HD).astype(jnp.float32)
    whole_cache = cache.reshape(LAYERS, ROWS, 2, KVH, CH, 2 * HD).transpose(0, 1, 3, 2, 4, 5)
    whole_cache = whole_cache.reshape(LAYERS, ROWS, KVH, 2 * CH, 2 * HD).astype(jnp.float32)
    cache_keys = whole_cache[..., :HD]
    cache_values = whole_cache[..., HD:]
    cache_scores = jnp.einsum('lsrgqd,lrgpd->lsrgqp', query_rows, cache_keys, precision=lax.Precision.HIGHEST) * score_scale
    cache_valid = jnp.arange(2 * CH).astype(jnp.int32)[None, :] < cache_lengths[:, None]
    cache_scores = jnp.where(cache_valid[None, None, :, None, None, :], cache_scores, NEG_FILL)
    fresh_scores = jnp.einsum('lsrgqd,lurgd->lsrgqu', query_rows, new_keys.astype(jnp.float32), precision=lax.Precision.HIGHEST) * score_scale
    fresh_valid = step_index[None, :] <= step_index[:, None]
    fresh_scores = jnp.where(fresh_valid[None, :, None, None, None, :], fresh_scores, NEG_FILL)
    all_scores = jnp.concatenate([cache_scores, fresh_scores], -1)
    row_max = lax.optimization_barrier(jnp.max(all_scores, -1, keepdims=True))
    weights = jnp.exp(all_scores - row_max)
    row_total = lax.optimization_barrier(jnp.sum(weights, -1))
    weighted = jnp.einsum('lsrgqp,lrgpd->lsrgqd', weights[..., :2 * CH], cache_values, precision=lax.Precision.HIGHEST)
    weighted = weighted + jnp.einsum('lsrgqu,lurgd->lsrgqd', weights[..., 2 * CH:], new_values.astype(jnp.float32), precision=lax.Precision.HIGHEST)
    result = (weighted / row_total[..., None]).astype(jnp.bfloat16)
    result = result.reshape(LAYERS, STEPS, ROWS, KVH, 2, 2, HD).transpose(0, 1, 2, 4, 3, 5, 6)
    attention_out = result.reshape(LAYERS, STEPS, ROWS, QH * HD)
    return (new_entries, attention_out)
```

```python
import functools
import math

import jax
import jax.numpy as jnp
from jax import lax
from jax.experimental import pallas as pl
from jax.experimental.pallas import tpu as pltpu
from jax.sharding import PartitionSpec as P

ROPE_BASE = 1000000.0
NEG_FILL = -1e30
MESH = pl.DeviceIdType.MESH
NT = (((1,), (1,)), ((), ()))
PAIRS = 8


def kernel(
    dims,
    lens_ref,
    hidden_ref,
    w_hbm,
    query_ref,
    cache_hbm,
    updated_ref,
    packed_ref,
    cos_ref,
    sin_ref,
    entries_ref,
    out_ref,
    w_buf,
    cache_buf,
    delta_buf,
    product,
    send_buf,
    sum_buf,
    piece_buf,
    other_piece,
    other_query,
    back_buf,
    back_stats,
    got_buf,
    got_stats,
    own_out,
    own_max,
    own_total,
    local_sem,
    cache_sem,
    delta_send,
    delta_recv,
    query_send,
    query_recv,
    sum_send,
    sum_recv,
    back_send,
    back_recv,
    tail_send,
    tail_recv,
):
    n_tp, n_pp, n_dp, heads, rows_dev, steps = dims
    n_all = n_tp * n_pp * n_dp
    head_dim = query_ref.shape[1]
    half_positions = cache_buf.shape[2]
    tokens, width = product.shape
    piece = width // n_tp
    group_rows = rows_dev * steps * 2
    blocks = group_rows // (16 * PAIRS)
    block_rows = 16 * PAIRS
    slot_rows = 16
    tp = lax.axis_index("tp")
    me = (tp * n_pp + lax.axis_index("pp")) * n_dp + lax.axis_index("dp")
    upper = tp // (n_tp // 2)
    partner = {"tp": lax.rem(tp + n_tp // 2, n_tp)}
    scale = 1.0 / math.sqrt(head_dim)

    w_copy = pltpu.make_async_copy(w_hbm, w_buf, local_sem.at[0])
    w_copy.start()

    def cache_copy(g):
        return pltpu.make_async_copy(cache_hbm.at[:, g], cache_buf.at[g], cache_sem.at[g])

    for g in range(heads):
        cache_copy(g).start()

    def place(index):
        return {
            "tp": index // (n_pp * n_dp),
            "pp": lax.rem(index // n_dp, n_pp),
            "dp": lax.rem(index, n_dp),
        }

    barrier = pltpu.get_barrier_semaphore()

    def greet(k, carry):
        pl.semaphore_signal(
            barrier, inc=1, device_id=place(lax.rem(me + k, n_all)), device_id_type=MESH
        )
        return carry

    lax.fori_loop(1, n_all, greet, 0)
    pl.semaphore_wait(barrier, n_all - 1)

    def owner_rows(index):
        return pl.ds(pl.multiple_of((index // n_dp) * slot_rows, slot_rows), slot_rows)

    my_rows = pl.ds(pl.multiple_of(me * slot_rows, slot_rows), slot_rows)

    def delta_copy(k):
        target = lax.rem(me + k, n_all)
        return pltpu.make_async_remote_copy(
            src_ref=packed_ref.at[owner_rows(target)],
            dst_ref=delta_buf.at[my_rows],
            send_sem=delta_send.at[k],
            recv_sem=delta_recv.at[k],
            device_id=place(target),
            device_id_type=MESH,
        )

    def start_delta(k, carry):
        delta_copy(k).start()
        return carry

    lax.fori_loop(1, n_all, start_delta, 0)
    own_delta = pltpu.make_async_copy(
        packed_ref.at[owner_rows(me)], delta_buf.at[my_rows], local_sem.at[1]
    )
    own_delta.start()

    def group_slice(g):
        return pl.ds(pl.multiple_of(g * group_rows, group_rows), group_rows)

    def query_copy(g):
        return pltpu.make_async_remote_copy(
            src_ref=query_ref.at[group_slice(g)],
            dst_ref=other_query.at[group_slice(g)],
            send_sem=query_send.at[g],
            recv_sem=query_recv.at[g],
            device_id=partner,
            device_id_type=MESH,
        )

    def back_copy(g):
        return pltpu.make_async_remote_copy(
            src_ref=back_buf.at[group_slice(g)],
            dst_ref=got_buf.at[group_slice(g)],
            send_sem=back_send.at[g],
            recv_sem=back_recv.at[g],
            device_id=partner,
            device_id_type=MESH,
        )

    for g in range(heads):
        query_copy(g).start()

    hidden = hidden_ref[...]
    w_copy.wait()
    tile = 256
    for c in range(width // tile):
        cols = slice(c * tile, (c + 1) * tile)
        product[:, cols] = jnp.dot(hidden, w_buf[:, cols], preferred_element_type=jnp.float32)

    def wait_delta(k, carry):
        delta_copy(k).wait()
        return carry

    lax.fori_loop(1, n_all, wait_delta, 0)
    own_delta.wait()
    shard_rows = hidden.shape[1]
    row_index = lax.broadcasted_iota(jnp.int32, (128, shard_rows), 1).astype(jnp.float32)
    taken = jnp.broadcast_to(updated_ref[...], (128, shard_rows)) == 1

    def add_deltas(chunk, carry):
        got = delta_buf[pl.ds(pl.multiple_of(chunk * 256, 256), 256), :].astype(jnp.float32)
        got = got.reshape(16, 16, 128)
        values = got[:, :8].reshape(128, 128)
        meta = got[:, 8:].reshape(128, 128)
        row = meta[:, 1:2] * 16.0 + meta[:, 2:3]
        place_row = jnp.where((row_index == row) & taken, meta[:, 0:1], 0.0).astype(jnp.bfloat16)
        picked = lax.dot_general(hidden, place_row, NT, preferred_element_type=jnp.float32)
        high = picked.astype(jnp.bfloat16)
        low = (picked - high.astype(jnp.float32)).astype(jnp.bfloat16)
        for c in range(width // tile):
            cols = slice(c * tile, (c + 1) * tile)
            spread = jnp.concatenate(
                [
                    jnp.where(meta[:, 3:4] == float(j), values, 0.0)
                    for j in range(c * tile // 128, (c + 1) * tile // 128)
                ],
                1,
            ).astype(jnp.bfloat16)
            product[:, cols] += jnp.dot(
                high, spread, preferred_element_type=jnp.float32
            ) + jnp.dot(low, spread, preferred_element_type=jnp.float32)
        return carry

    lax.fori_loop(0, n_all // 16, add_deltas, 0)
    for j in range(n_tp):
        send_buf[j] = product[:, j * piece : (j + 1) * piece].astype(jnp.bfloat16)

    def sum_copy(k):
        target = lax.rem(tp + k, n_tp)
        return pltpu.make_async_remote_copy(
            src_ref=send_buf.at[target],
            dst_ref=sum_buf.at[k],
            send_sem=sum_send.at[k],
            recv_sem=sum_recv.at[k],
            device_id={"tp": target},
            device_id_type=MESH,
        )

    for k in range(1, n_tp):
        sum_copy(k).start()

    row16 = lax.broadcasted_iota(jnp.int32, (16, 256), 0)
    col16 = lax.broadcasted_iota(jnp.int32, (16, 256), 1)
    same = (row16 // 8) == (col16 // 128)
    position = lax.rem(col16, 128) + upper * half_positions
    eye = lax.broadcasted_iota(jnp.int32, (128, 128), 0) == lax.broadcasted_iota(
        jnp.int32, (128, 128), 1
    )

    def attend(source, g, block):
        base = block * 2 * PAIRS
        scores, valids = [], []
        start = pl.multiple_of(g * group_rows + block * block_rows, block_rows)
        for i in range(PAIRS):
            r = base + 2 * i
            keys = jnp.concatenate(
                [cache_buf[g, r, :, :head_dim], cache_buf[g, r + 1, :, :head_dim]], 0
            )
            q16 = source[pl.ds(start + 16 * i, 16), :]
            scores.append(lax.dot_general(q16, keys, NT, preferred_element_type=jnp.float32))
            length = jnp.where(row16 < 8, lens_ref[r], lens_ref[r + 1])
            valids.append(same & (position < length))
        maxima, totals, outs = [], [], []
        for i in range(PAIRS):
            r = base + 2 * i
            s = jnp.where(valids[i], scores[i] * scale, NEG_FILL)
            m = jnp.max(s, -1, keepdims=True)
            e = jnp.where(valids[i], jnp.exp(s - m), 0.0)
            maxima.append(m)
            totals.append(jnp.sum(e, -1, keepdims=True))
            values = jnp.concatenate(
                [cache_buf[g, r, :, head_dim:], cache_buf[g, r + 1, :, head_dim:]], 0
            )
            outs.append(
                jnp.dot(e.astype(jnp.bfloat16), values, preferred_element_type=jnp.float32)
            )
        return (
            start,
            jnp.concatenate(maxima, 0),
            jnp.concatenate(totals, 0),
            jnp.concatenate(outs, 0),
        )

    for g in range(heads):
        cache_copy(g).wait()

    def own_group(g, carry):
        for block in range(blocks):
            start, m, l, o = attend(query_ref, g, block)
            where = pl.ds(start, block_rows)
            own_out[where, :] = o
            own_max[where, :] = jnp.broadcast_to(m, (block_rows, 128))
            own_total[where, :] = jnp.broadcast_to(l, (block_rows, 128))
        return carry

    lax.fori_loop(0, heads, own_group, 0)

    def other_group(g, carry):
        query_copy(g).wait()
        for block in range(blocks):
            start, m, l, o = attend(other_query, g, block)
            back_buf[pl.ds(start, block_rows), :] = o.astype(jnp.bfloat16)
            at = pl.ds(g * blocks + block, 1)
            back_stats[0, at, :] = jnp.sum(jnp.where(eye, m, 0.0), 0, keepdims=True)
            back_stats[1, at, :] = jnp.sum(jnp.where(eye, l, 0.0), 0, keepdims=True)
        back_copy(g).start()
        return carry

    lax.fori_loop(0, heads, other_group, 0)
    stats_copy = pltpu.make_async_remote_copy(
        src_ref=back_stats,
        dst_ref=got_stats,
        send_sem=tail_send.at[0],
        recv_sem=tail_recv.at[0],
        device_id=partner,
        device_id_type=MESH,
    )
    stats_copy.start()

    for k in range(1, n_tp):
        sum_copy(k).wait()
    total = send_buf[tp].astype(jnp.float32)
    for k in range(1, n_tp):
        total += sum_buf[k].astype(jnp.float32)
    cosine, sine = cos_ref[...], sin_ref[...]
    for g in range(heads):
        x = total[:, g * head_dim : (g + 1) * head_dim]
        turned = x * cosine + pltpu.roll(x, head_dim // 2, 1) * sine
        piece_buf[:, g * head_dim : (g + 1) * head_dim] = jnp.where(upper == 0, turned, x).astype(
            jnp.bfloat16
        )
    piece_copy = pltpu.make_async_remote_copy(
        src_ref=piece_buf,
        dst_ref=other_piece,
        send_sem=tail_send.at[1],
        recv_sem=tail_recv.at[1],
        device_id=partner,
        device_id_type=MESH,
    )
    piece_copy.start()
    entries_ref[...] = piece_buf[...]
    piece_copy.wait()
    stats_copy.wait()

    q_row = lax.broadcasted_iota(jnp.int32, (block_rows, tokens), 0)
    k_col = lax.broadcasted_iota(jnp.int32, (block_rows, tokens), 1)
    for g in range(heads):
        cols = slice(g * head_dim, (g + 1) * head_dim)
        mine, theirs = piece_buf[:, cols], other_piece[:, cols]
        new_keys = jnp.where(upper == 0, mine, theirs)
        new_values = jnp.where(upper == 0, theirs, mine)
        back_copy(g).wait()
        for block in range(blocks):
            where = slice(g * group_rows + block * block_rows, g * group_rows + (block + 1) * block_rows)
            row_of = block * (block_rows // (2 * steps)) + q_row // (2 * steps)
            step_of = lax.rem(q_row, 2 * steps) // 2
            valid = (row_of == lax.rem(k_col, rows_dev)) & (k_col // rows_dev <= step_of)
            s = lax.dot_general(query_ref[where, :], new_keys, NT, preferred_element_type=jnp.float32)
            s = jnp.where(valid, s * scale, NEG_FILL)
            m3 = jnp.max(s, -1, keepdims=True)
            e = jnp.where(valid, jnp.exp(s - m3), 0.0)
            l3 = jnp.sum(e, -1, keepdims=True)
            o3 = jnp.dot(e.astype(jnp.bfloat16), new_values, preferred_element_type=jnp.float32)
            at = g * blocks + block
            m2 = jnp.sum(jnp.where(eye, got_stats[0, at : at + 1, :], 0.0), -1, keepdims=True)
            l2 = jnp.sum(jnp.where(eye, got_stats[1, at : at + 1, :], 0.0), -1, keepdims=True)
            m1, l1 = own_max[where, 0:1], own_total[where, 0:1]
            top = jnp.maximum(jnp.maximum(m1, m2), m3)
            f1, f2, f3 = jnp.exp(m1 - top), jnp.exp(m2 - top), jnp.exp(m3 - top)
            whole = own_out[where, :] * f1 + got_buf[where, :].astype(jnp.float32) * f2 + o3 * f3
            out_ref[where, :] = (whole / (l1 * f1 + l2 * f2 + l3 * f3)).astype(jnp.bfloat16)


def shards(
    sizes,
    hidden,
    w_kv,
    queries,
    cache,
    cache_lengths,
    updated,
    delta_values,
    delta_scales,
    delta_targets,
    send_counts,
):
    n_tp, n_pp, n_dp = sizes
    n_all = n_tp * n_pp * n_dp
    owners, slots, block_width = delta_values.shape[1:]
    shard_rows, width = w_kv.shape[1:]
    steps, rows_dev = hidden.shape[1:3]
    heads, half_positions = cache.shape[2:4]
    head_dim = cache.shape[4] // 2
    tokens = steps * rows_dev
    piece = width // n_tp
    all_queries = heads * rows_dev * steps * 2
    bf16, f32 = jnp.bfloat16, jnp.float32

    live = jnp.arange(slots, dtype=jnp.int32)[None, :] < send_counts[0][:, None]
    scales = jnp.where(live, delta_scales[0], jnp.zeros((), bf16))
    row_blocks = width // block_width
    target = delta_targets[0]
    row = target // row_blocks
    fields = (scales, (row // 16).astype(bf16), (row % 16).astype(bf16), (target % row_blocks).astype(bf16))
    lane = jnp.arange(block_width, dtype=jnp.int32)
    meta = jnp.zeros((owners, slots, block_width), bf16)
    for i, field in enumerate(fields):
        meta = jnp.where(lane == i, field[..., None], meta)
    packed = jnp.concatenate([delta_values[0], meta], 1).reshape(owners * 2 * slots, block_width)

    query_rows = queries[0].reshape(steps, rows_dev, heads, 2, head_dim)
    query_rows = query_rows.transpose(2, 1, 0, 3, 4).reshape(all_queries, head_dim)

    positions = cache_lengths[None, :] + jnp.arange(steps, dtype=jnp.int32)[:, None]
    half = head_dim // 2
    inverse = jnp.exp(
        jnp.arange(half).astype(f32) * (-2.0 / head_dim) * math.log(ROPE_BASE)
    )
    angles = positions.astype(f32).reshape(tokens, 1) * inverse
    cosine, sine = jnp.cos(angles), jnp.sin(angles)
    cosine = jnp.concatenate([cosine, cosine], 1)
    sine = jnp.concatenate([-sine, sine], 1)

    vmem = pl.BlockSpec(memory_space=pltpu.VMEM)
    anywhere = pl.BlockSpec(memory_space=pl.ANY)
    stat_rows = max(8, all_queries // 128)
    dma = pltpu.SemaphoreType.DMA
    entries, attended = pl.pallas_call(
        functools.partial(kernel, (n_tp, n_pp, n_dp, heads, rows_dev, steps)),
        out_shape=(
            jax.ShapeDtypeStruct((tokens, piece), bf16),
            jax.ShapeDtypeStruct((all_queries, head_dim), bf16),
        ),
        in_specs=[
            pl.BlockSpec(memory_space=pltpu.SMEM),
            vmem,
            anywhere,
            vmem,
            anywhere,
            vmem,
            vmem,
            vmem,
            vmem,
        ],
        out_specs=(vmem, vmem),
        scratch_shapes=[
            pltpu.VMEM((shard_rows, width), bf16),
            pltpu.VMEM((heads, rows_dev, half_positions, 2 * head_dim), bf16),
            pltpu.VMEM((n_all * 2 * slots, block_width), bf16),
            pltpu.VMEM((tokens, width), f32),
            pltpu.VMEM((n_tp, tokens, piece), bf16),
            pltpu.VMEM((n_tp, tokens, piece), bf16),
            pltpu.VMEM((tokens, piece), bf16),
            pltpu.VMEM((tokens, piece), bf16),
            pltpu.VMEM((all_queries, head_dim), bf16),
            pltpu.VMEM((all_queries, head_dim), bf16),
            pltpu.VMEM((2, stat_rows, 128), f32),
            pltpu.VMEM((all_queries, head_dim), bf16),
            pltpu.VMEM((2, stat_rows, 128), f32),
            pltpu.VMEM((all_queries, head_dim), f32),
            pltpu.VMEM((all_queries, 128), f32),
            pltpu.VMEM((all_queries, 128), f32),
            dma((2,)),
            dma((heads,)),
            dma((n_all,)),
            dma((n_all,)),
            dma((heads,)),
            dma((heads,)),
            dma((n_tp,)),
            dma((n_tp,)),
            dma((heads,)),
            dma((heads,)),
            dma((2,)),
            dma((2,)),
        ],
        compiler_params=pltpu.CompilerParams(
            collective_id=0, has_side_effects=True, vmem_limit_bytes=48 * 1024 * 1024
        ),
        name="decode",
    )(
        cache_lengths,
        hidden[0].reshape(tokens, shard_rows),
        w_kv[0],
        query_rows,
        cache[0],
        updated,
        packed,
        cosine,
        sine,
    )
    attended = attended.reshape(heads, rows_dev, steps, 2, head_dim).transpose(2, 1, 0, 3, 4)
    return (
        entries.reshape(1, steps, rows_dev, piece),
        attended.reshape(1, steps, rows_dev, heads * 2 * head_dim),
    )


def solution(mesh):
    placed = (
        P(("groups", "pp"), None, "dp", "tp"),
        P(("groups", "pp"), "tp", None),
        P(("groups", "pp"), None, "dp", "tp"),
        P(("groups", "pp"), "dp", "tp", None, None),
        P(("groups", "dp")),
        P(("groups", "pp"), "tp"),
        P(("groups", "tp", "pp", "dp"), None, None, None),
        P(("groups", "tp", "pp", "dp"), None, None),
        P(("groups", "tp", "pp", "dp"), None, None),
        P(("groups", "tp", "pp", "dp"), None),
    )
    sizes = (mesh.shape["tp"], mesh.shape["pp"], mesh.shape["dp"])
    return jax.shard_map(
        functools.partial(shards, sizes),
        mesh=mesh,
        in_specs=placed,
        out_specs=(P(("groups", "pp"), None, "dp", "tp"), P(("groups", "pp"), None, "dp", "tp")),
        check_vma=False,
    )
```

```python
import functools
import math

import jax
import jax.numpy as jnp
from jax import lax
from jax.experimental import pallas as pl
from jax.experimental.pallas import tpu as pltpu
from jax.sharding import PartitionSpec as P

ROPE_BASE = 1000000.0
NEG_FILL = -1e30
MESH = pl.DeviceIdType.MESH
NT = (((1,), (1,)), ((), ()))
PAIRS = 8


def kernel(
    dims,
    lens_hbm,
    hidden_hbm,
    w_hbm,
    query_hbm,
    cache_hbm,
    updated_hbm,
    values_hbm,
    scales_hbm,
    targets_hbm,
    counts_hbm,
    entries_ref,
    out_ref,
    lens_ref,
    lens_row,
    hidden_ref,
    w_buf,
    query_raw,
    cache_buf,
    updated_ref,
    values_ref,
    scales_ref,
    targets_ref,
    counts_ref,
    scales_wide,
    packed_ref,
    query_wide,
    query_ref,
    cos_ref,
    sin_ref,
    delta_buf,
    product,
    send_buf,
    sum_buf,
    pair_buf,
    pair_got,
    kept_sum,
    piece_buf,
    other_piece,
    other_query,
    back_buf,
    back_stats,
    got_buf,
    got_stats,
    own_out,
    own_max,
    own_total,
    local_sem,
    cache_sem,
    delta_send,
    delta_recv,
    query_send,
    query_recv,
    sum_send,
    sum_recv,
    back_send,
    back_recv,
    tail_send,
    tail_recv,
):
    n_tp, n_pp, n_dp, row_blocks = dims
    n_all = n_tp * n_pp * n_dp
    n_half = n_tp // 2
    heads, rows_dev, half_positions, head_dim = cache_buf.shape
    head_dim = head_dim // 2
    tokens, width = product.shape
    steps = tokens // rows_dev
    owners, slots = targets_ref.shape
    piece = width // n_tp
    row_queries = 2 * steps
    group_rows = rows_dev * row_queries
    blocks = group_rows // (16 * PAIRS)
    block_rows = 16 * PAIRS
    slot_rows = 16
    tp = lax.axis_index("tp")
    me = (tp * n_pp + lax.axis_index("pp")) * n_dp + lax.axis_index("dp")
    upper = tp // n_half
    place_in_half = lax.rem(tp, n_half)
    partner = {"tp": lax.rem(tp + n_half, n_tp)}
    scale = 1.0 / math.sqrt(head_dim)
    f32, bf16 = jnp.float32, jnp.bfloat16

    def load(i, source, target):
        copy = pltpu.make_async_copy(source, target, local_sem.at[i])
        copy.start()
        return copy

    small = [
        load(2, scales_hbm, scales_ref),
        load(3, targets_hbm, targets_ref),
        load(4, counts_hbm, counts_ref),
        load(5, values_hbm, values_ref),
    ]
    query_load = load(6, query_hbm, query_raw)
    hidden_load = load(7, hidden_hbm, hidden_ref)
    later = [
        load(8, updated_hbm, updated_ref),
        load(9, lens_hbm, lens_ref),
        load(10, lens_hbm, lens_row),
    ]
    w_copy = load(0, w_hbm, w_buf)

    def cache_copy(g):
        return pltpu.make_async_copy(cache_hbm.at[:, g], cache_buf.at[g], cache_sem.at[g])

    for g in range(heads):
        cache_copy(g).start()

    def place(index):
        return {
            "tp": index // (n_pp * n_dp),
            "pp": lax.rem(index // n_dp, n_pp),
            "dp": lax.rem(index, n_dp),
        }

    barrier = pltpu.get_barrier_semaphore()

    def greet(k, carry):
        pl.semaphore_signal(
            barrier, inc=1, device_id=place(lax.rem(me + k, n_all)), device_id_type=MESH
        )
        return carry

    lax.fori_loop(1, n_all, greet, 0)

    query_load.wait()
    for g in range(heads):
        for t in range(steps):
            for b in range(2):
                lanes = slice((g * 2 + b) * head_dim, (g * 2 + b + 1) * head_dim)
                query_wide[pl.ds(g * group_rows + t * 2 + b, rows_dev, stride=row_queries), :] = (
                    query_raw[t, :, lanes].astype(f32)
                )
    query_ref[...] = query_wide[...].astype(bf16)

    for copy in small:
        copy.wait()
    scales_wide[...] = scales_ref[...].astype(f32)
    row8 = lax.broadcasted_iota(jnp.int32, (slots, slots), 0)
    col8 = lax.broadcasted_iota(jnp.int32, (slots, slots), 1)
    lane = lax.broadcasted_iota(jnp.int32, (slots, 128), 1)
    owner_lane = lax.broadcasted_iota(jnp.int32, counts_ref.shape, 1)

    def pack(o, carry):
        def column(x):
            wide = jnp.where(row8 == col8, jnp.broadcast_to(x, (slots, slots)), 0.0)
            return jnp.sum(wide, -1, keepdims=True)

        count = jnp.sum(jnp.where(owner_lane == o, counts_ref[...].astype(f32), 0.0), -1, keepdims=True)
        scales = scales_wide[pl.ds(o, 1), :]
        scales = jnp.where(col8[:1].astype(f32) < count, scales, 0.0)
        target = targets_ref[pl.ds(o, 1), :]
        shift = row_blocks.bit_length() - 1
        high = (target >> (shift + 4)).astype(f32)
        low = ((target >> shift) & 15).astype(f32)
        block = (target & (row_blocks - 1)).astype(f32)
        meta = jnp.zeros((slots, 128), f32)
        for i, field in enumerate((scales, high, low, block)):
            meta = jnp.where(lane == i, column(field), meta)
        both = jnp.concatenate([values_ref[o].astype(f32), meta], 0)
        packed_ref[pl.ds(pl.multiple_of(o * slot_rows, slot_rows), slot_rows), :] = both.astype(bf16)
        return carry

    lax.fori_loop(0, owners, pack, 0)
    pl.semaphore_wait(barrier, n_all - 1)

    def owner_rows(index):
        return pl.ds(pl.multiple_of((index // n_dp) * slot_rows, slot_rows), slot_rows)

    my_rows = pl.ds(pl.multiple_of(me * slot_rows, slot_rows), slot_rows)

    def delta_copy(k):
        target = lax.rem(me + k, n_all)
        return pltpu.make_async_remote_copy(
            src_ref=packed_ref.at[owner_rows(target)],
            dst_ref=delta_buf.at[my_rows],
            send_sem=delta_send.at[k],
            recv_sem=delta_recv.at[k],
            device_id=place(target),
            device_id_type=MESH,
        )

    def group_slice(g):
        return pl.ds(pl.multiple_of(g * group_rows, group_rows), group_rows)

    def query_copy(g):
        return pltpu.make_async_remote_copy(
            src_ref=query_ref.at[group_slice(g)],
            dst_ref=other_query.at[group_slice(g)],
            send_sem=query_send.at[g],
            recv_sem=query_recv.at[g],
            device_id=partner,
            device_id_type=MESH,
        )

    def back_copy(g):
        return pltpu.make_async_remote_copy(
            src_ref=back_buf.at[group_slice(g)],
            dst_ref=got_buf.at[group_slice(g)],
            send_sem=back_send.at[g],
            recv_sem=back_recv.at[g],
            device_id=partner,
            device_id_type=MESH,
        )

    def start_delta(k, carry):
        delta_copy(k).start()
        return carry

    query_copy(0).start()
    lax.fori_loop(1, n_all, start_delta, 0)
    own_delta = pltpu.make_async_copy(
        packed_ref.at[owner_rows(me)], delta_buf.at[my_rows], local_sem.at[1]
    )
    own_delta.start()
    for g in range(1, heads):
        query_copy(g).start()

    hidden_load.wait()
    hidden = hidden_ref[...]
    w_copy.wait()
    tile = 256
    for c in range(width // tile):
        cols = slice(c * tile, (c + 1) * tile)
        product[:, cols] = jnp.dot(hidden, w_buf[:, cols], preferred_element_type=f32)

    for copy in later:
        copy.wait()

    def wait_delta(k, carry):
        delta_copy(k).wait()
        return carry

    lax.fori_loop(1, n_all, wait_delta, 0)
    own_delta.wait()
    shard_rows = hidden.shape[1]
    row_index = lax.broadcasted_iota(jnp.int32, (128, shard_rows), 1).astype(f32)
    taken = jnp.broadcast_to(updated_ref[...], (128, shard_rows)) == 1

    def add_deltas(chunk, carry):
        got = delta_buf[pl.ds(pl.multiple_of(chunk * 256, 256), 256), :].astype(f32)
        got = got.reshape(16, 16, 128)
        values = got[:, :8].reshape(128, 128)
        meta = got[:, 8:].reshape(128, 128)
        row = meta[:, 1:2] * 16.0 + meta[:, 2:3]
        place_row = jnp.where((row_index == row) & taken, meta[:, 0:1], 0.0).astype(bf16)
        picked = lax.dot_general(hidden, place_row, NT, preferred_element_type=f32)
        high = picked.astype(bf16)
        low = (picked - high.astype(f32)).astype(bf16)
        for c in range(width // tile):
            cols = slice(c * tile, (c + 1) * tile)
            spread = jnp.concatenate(
                [
                    jnp.where(meta[:, 3:4] == float(j), values, 0.0)
                    for j in range(c * tile // 128, (c + 1) * tile // 128)
                ],
                1,
            ).astype(bf16)
            product[:, cols] += jnp.dot(high, spread, preferred_element_type=f32) + jnp.dot(
                low, spread, preferred_element_type=f32
            )
        return carry

    lax.fori_loop(0, n_all // 16, add_deltas, 0)
    for j in range(n_half):
        for part in range(2):
            i = part * n_half + j
            send_buf[j, part] = product[:, i * piece : (i + 1) * piece].astype(bf16)

    def sum_copy(k):
        target = lax.rem(place_in_half + k, n_half)
        return pltpu.make_async_remote_copy(
            src_ref=send_buf.at[target],
            dst_ref=sum_buf.at[k],
            send_sem=sum_send.at[k],
            recv_sem=sum_recv.at[k],
            device_id={"tp": upper * n_half + target},
            device_id_type=MESH,
        )

    for k in range(1, n_half):
        sum_copy(k).start()

    def tail_copy(i, source, target):
        return pltpu.make_async_remote_copy(
            src_ref=source,
            dst_ref=target,
            send_sem=tail_send.at[i],
            recv_sem=tail_recv.at[i],
            device_id=partner,
            device_id_type=MESH,
        )

    row16 = lax.broadcasted_iota(jnp.int32, (16, 256), 0)
    col16 = lax.broadcasted_iota(jnp.int32, (16, 256), 1)
    same = (row16 // 8) == (col16 // 128)
    position = lax.rem(col16, 128) + upper * half_positions
    eye = lax.broadcasted_iota(jnp.int32, (128, 128), 0) == lax.broadcasted_iota(
        jnp.int32, (128, 128), 1
    )

    def attend(source, g, block):
        base = block * 2 * PAIRS
        scores, valids = [], []
        start = pl.multiple_of(g * group_rows + block * block_rows, block_rows)
        for i in range(PAIRS):
            r = base + 2 * i
            keys = jnp.concatenate(
                [cache_buf[g, r, :, :head_dim], cache_buf[g, r + 1, :, :head_dim]], 0
            )
            q16 = source[pl.ds(start + 16 * i, 16), :]
            scores.append(lax.dot_general(q16, keys, NT, preferred_element_type=f32))
            length = jnp.where(row16 < 8, lens_ref[r], lens_ref[r + 1])
            valids.append(same & (position < length))
        maxima, totals, outs = [], [], []
        for i in range(PAIRS):
            r = base + 2 * i
            s = jnp.where(valids[i], scores[i] * scale, NEG_FILL)
            m = jnp.max(s, -1, keepdims=True)
            e = jnp.where(valids[i], jnp.exp(s - m), 0.0)
            maxima.append(m)
            totals.append(jnp.sum(e, -1, keepdims=True))
            values = jnp.concatenate(
                [cache_buf[g, r, :, head_dim:], cache_buf[g, r + 1, :, head_dim:]], 0
            )
            outs.append(jnp.dot(e.astype(bf16), values, preferred_element_type=f32))
        return (
            start,
            jnp.concatenate(maxima, 0),
            jnp.concatenate(totals, 0),
            jnp.concatenate(outs, 0),
        )

    def other_group(g, carry):
        cache_copy(g).wait()
        query_copy(g).wait()
        for block in range(blocks):
            start, m, l, o = attend(other_query, g, block)
            back_buf[pl.ds(start, block_rows), :] = o.astype(bf16)
            at = pl.ds(g * blocks + block, 1)
            back_stats[0, at, :] = jnp.sum(jnp.where(eye, m, 0.0), 0, keepdims=True)
            back_stats[1, at, :] = jnp.sum(jnp.where(eye, l, 0.0), 0, keepdims=True)
        back_copy(g).start()
        return carry

    to_column = lax.broadcasted_iota(jnp.int32, (rows_dev, rows_dev), 0) == lax.broadcasted_iota(
        jnp.int32, (rows_dev, rows_dev), 1
    )
    lengths = jnp.broadcast_to(lens_row[...].astype(f32).reshape(1, rows_dev), (rows_dev, rows_dev))
    lengths = jnp.sum(jnp.where(to_column, lengths, 0.0), -1, keepdims=True)
    index = lax.rem(lax.broadcasted_iota(jnp.int32, (1, head_dim), 1), head_dim // 2).astype(f32)
    inverse = jnp.exp(index * (-2.0 / head_dim) * math.log(ROPE_BASE))
    positions = jnp.concatenate([lengths + float(t) for t in range(steps)], 0)
    angles = positions * inverse
    first = lax.broadcasted_iota(jnp.int32, (tokens, head_dim), 1) < head_dim // 2
    sine = jnp.sin(angles)
    cos_ref[...] = jnp.cos(angles)
    sin_ref[...] = jnp.where(first, -sine, sine)

    early = (heads + 1) // 2
    lax.fori_loop(0, early, other_group, 0)

    for k in range(1, n_half):
        sum_copy(k).wait()
    sums = []
    for part in range(2):
        total = send_buf[place_in_half, part].astype(f32)
        for k in range(1, n_half):
            total += sum_buf[k, part].astype(f32)
        sums.append(total)
    kept_sum[...] = jnp.where(upper == 0, sums[0], sums[1])
    pair_buf[...] = jnp.where(upper == 0, sums[1], sums[0]).astype(bf16)
    pair_copy = tail_copy(2, pair_buf, pair_got)
    pair_copy.start()

    lax.fori_loop(early, heads, other_group, 0)
    stats_copy = tail_copy(0, back_stats, got_stats)
    stats_copy.start()

    pair_copy.wait()
    for g in range(heads):
        cols = slice(g * head_dim, (g + 1) * head_dim)
        x = kept_sum[:, cols] + pair_got[:, cols].astype(f32)
        turned = x * cos_ref[...] + pltpu.roll(x, head_dim // 2, 1) * sin_ref[...]
        piece_buf[:, cols] = jnp.where(upper == 0, turned, x).astype(bf16)
    piece_copy = tail_copy(1, piece_buf, other_piece)
    piece_copy.start()
    entries_ref[...] = piece_buf[...]

    def own_group(g, carry):
        for block in range(blocks):
            start, m, l, o = attend(query_ref, g, block)
            where = pl.ds(start, block_rows)
            own_out[where, :] = o
            own_max[where, :] = jnp.broadcast_to(m, (block_rows, 128))
            own_total[where, :] = jnp.broadcast_to(l, (block_rows, 128))
        return carry

    lax.fori_loop(0, heads, own_group, 0)
    piece_copy.wait()

    q_row = lax.broadcasted_iota(jnp.int32, (block_rows, tokens), 0)
    k_col = lax.broadcasted_iota(jnp.int32, (block_rows, tokens), 1)
    step_of = lax.rem(q_row, row_queries) // 2
    seen = k_col // rows_dev <= step_of
    for g in range(heads):
        cols = slice(g * head_dim, (g + 1) * head_dim)
        mine, theirs = piece_buf[:, cols], other_piece[:, cols]
        new_keys = jnp.where(upper == 0, mine, theirs)
        new_values = jnp.where(upper == 0, theirs, mine)
        for block in range(blocks):
            first_row = g * group_rows + block * block_rows
            where = slice(first_row, first_row + block_rows)
            row_of = block * (block_rows // row_queries) + q_row // row_queries
            valid = (row_of == lax.rem(k_col, rows_dev)) & seen
            s = lax.dot_general(query_ref[where, :], new_keys, NT, preferred_element_type=f32)
            s = jnp.where(valid, s * scale, NEG_FILL)
            m1, l1 = own_max[where, :], own_total[where, :]
            top = jnp.maximum(jnp.max(s, -1, keepdims=True), m1)
            e = jnp.where(valid, jnp.exp(s - top), 0.0)
            o3 = jnp.dot(e.astype(bf16), new_values, preferred_element_type=f32)
            f1 = jnp.exp(m1 - top)
            own_out[where, :] = own_out[where, :] * f1 + o3
            own_total[where, :] = l1 * f1 + jnp.sum(e, -1, keepdims=True)
            own_max[where, :] = top

    stats_copy.wait()
    for g in range(heads):
        back_copy(g).wait()
        for block in range(blocks):
            first_row = g * group_rows + block * block_rows
            where = slice(first_row, first_row + block_rows)
            at = g * blocks + block
            m2 = jnp.sum(jnp.where(eye, got_stats[0, at : at + 1, :], 0.0), -1, keepdims=True)
            l2 = jnp.sum(jnp.where(eye, got_stats[1, at : at + 1, :], 0.0), -1, keepdims=True)
            m1 = own_max[where, :]
            top = jnp.maximum(m1, m2)
            f1, f2 = jnp.exp(m1 - top), jnp.exp(m2 - top)
            whole = own_out[where, :] * f1 + got_buf[where, :].astype(f32) * f2
            query_wide[where, :] = whole / (own_total[where, :] * f1 + l2 * f2)
        for t in range(steps):
            for b in range(2):
                lanes = slice((g * 2 + b) * head_dim, (g * 2 + b + 1) * head_dim)
                rows = pl.ds(g * group_rows + t * 2 + b, rows_dev, stride=row_queries)
                out_ref[t, :, lanes] = query_wide[rows, :].astype(bf16)


def shards(
    sizes,
    hidden,
    w_kv,
    queries,
    cache,
    cache_lengths,
    updated,
    delta_values,
    delta_scales,
    delta_targets,
    send_counts,
):
    n_tp, n_pp, n_dp = sizes
    n_all = n_tp * n_pp * n_dp
    owners, slots, block_width = delta_values.shape[1:]
    shard_rows, width = w_kv.shape[1:]
    steps, rows_dev = hidden.shape[1:3]
    heads, half_positions = cache.shape[2:4]
    head_dim = cache.shape[4] // 2
    tokens = steps * rows_dev
    piece = width // n_tp
    all_queries = heads * rows_dev * steps * 2
    bf16, f32, i32 = jnp.bfloat16, jnp.float32, jnp.int32

    vmem = pl.BlockSpec(memory_space=pltpu.VMEM)
    anywhere = pl.BlockSpec(memory_space=pl.ANY)
    stat_rows = max(8, all_queries // 128)
    dma = pltpu.SemaphoreType.DMA
    rows = pltpu.VMEM((all_queries, head_dim), bf16)
    wide_rows = pltpu.VMEM((all_queries, head_dim), f32)
    stats = pltpu.VMEM((2, stat_rows, 128), f32)
    one_piece = pltpu.VMEM((tokens, piece), bf16)
    table = pltpu.VMEM((tokens, head_dim), f32)
    entries, attended = pl.pallas_call(
        functools.partial(kernel, (n_tp, n_pp, n_dp, width // block_width)),
        out_shape=(
            jax.ShapeDtypeStruct((tokens, piece), bf16),
            jax.ShapeDtypeStruct((steps, rows_dev, heads * 2 * head_dim), bf16),
        ),
        in_specs=[anywhere] * 10,
        out_specs=(vmem, vmem),
        scratch_shapes=[
            pltpu.SMEM((rows_dev,), i32),
            pltpu.VMEM((rows_dev,), i32),
            pltpu.VMEM((tokens, shard_rows), bf16),
            pltpu.VMEM((shard_rows, width), bf16),
            pltpu.VMEM((steps, rows_dev, heads * 2 * head_dim), bf16),
            pltpu.VMEM((heads, rows_dev, half_positions, 2 * head_dim), bf16),
            pltpu.VMEM((1, shard_rows), i32),
            pltpu.VMEM((owners, slots, block_width), bf16),
            pltpu.VMEM((owners, slots), bf16),
            pltpu.VMEM((owners, slots), i32),
            pltpu.VMEM((1, owners), i32),
            pltpu.VMEM((owners, slots), f32),
            pltpu.VMEM((owners * 2 * slots, block_width), bf16),
            wide_rows,
            rows,
            table,
            table,
            pltpu.VMEM((n_all * 2 * slots, block_width), bf16),
            pltpu.VMEM((tokens, width), f32),
            pltpu.VMEM((n_tp // 2, 2, tokens, piece), bf16),
            pltpu.VMEM((n_tp // 2, 2, tokens, piece), bf16),
            one_piece,
            one_piece,
            pltpu.VMEM((tokens, piece), f32),
            one_piece,
            one_piece,
            rows,
            rows,
            stats,
            rows,
            stats,
            wide_rows,
            wide_rows,
            wide_rows,
            dma((11,)),
            dma((heads,)),
            dma((n_all,)),
            dma((n_all,)),
            dma((heads,)),
            dma((heads,)),
            dma((n_tp // 2,)),
            dma((n_tp // 2,)),
            dma((heads,)),
            dma((heads,)),
            dma((3,)),
            dma((3,)),
        ],
        compiler_params=pltpu.CompilerParams(
            collective_id=0, has_side_effects=True, vmem_limit_bytes=56 * 1024 * 1024
        ),
        name="decode",
    )(
        cache_lengths,
        hidden[0].reshape(tokens, shard_rows),
        w_kv[0],
        queries[0],
        cache[0],
        updated,
        delta_values[0],
        delta_scales[0],
        delta_targets[0],
        send_counts,
    )
    return (entries.reshape(1, steps, rows_dev, piece), attended[None])


def solution(mesh):
    placed = (
        P(("groups", "pp"), None, "dp", "tp"),
        P(("groups", "pp"), "tp", None),
        P(("groups", "pp"), None, "dp", "tp"),
        P(("groups", "pp"), "dp", "tp", None, None),
        P(("groups", "dp")),
        P(("groups", "pp"), "tp"),
        P(("groups", "tp", "pp", "dp"), None, None, None),
        P(("groups", "tp", "pp", "dp"), None, None),
        P(("groups", "tp", "pp", "dp"), None, None),
        P(("groups", "tp", "pp", "dp"), None),
    )
    sizes = (mesh.shape["tp"], mesh.shape["pp"], mesh.shape["dp"])
    return jax.shard_map(
        functools.partial(shards, sizes),
        mesh=mesh,
        in_specs=placed,
        out_specs=(P(("groups", "pp"), None, "dp", "tp"), P(("groups", "pp"), None, "dp", "tp")),
        check_vma=False,
    )
```

```python
import functools
import math

import jax
import jax.numpy as jnp
from jax import lax
from jax.experimental import pallas as pl
from jax.experimental.pallas import tpu as pltpu
from jax.sharding import PartitionSpec as P

ROPE_BASE = 1000000.0
NEG_FILL = -1e30
MESH = pl.DeviceIdType.MESH
NT = (((1,), (1,)), ((), ()))
PAIRS = 8


def kernel(
    dims,
    lens_hbm,
    hidden_hbm,
    w_hbm,
    query_hbm,
    cache_hbm,
    updated_hbm,
    values_hbm,
    scales_hbm,
    targets_hbm,
    counts_hbm,
    entries_ref,
    out_ref,
    lens_ref,
    lens_row,
    hidden_ref,
    w_buf,
    query_raw,
    cache_buf,
    updated_ref,
    values_ref,
    scales_ref,
    targets_ref,
    counts_ref,
    scales_wide,
    packed_ref,
    query_wide,
    query_ref,
    cos_ref,
    sin_ref,
    delta_buf,
    product,
    send_buf,
    sum_buf,
    pair_buf,
    pair_got,
    kept_sum,
    piece_buf,
    other_piece,
    other_query,
    back_buf,
    back_stats,
    got_buf,
    got_stats,
    own_out,
    own_max,
    own_total,
    local_sem,
    cache_sem,
    delta_send,
    delta_recv,
    query_send,
    query_recv,
    sum_send,
    sum_recv,
    back_send,
    back_recv,
    tail_send,
    tail_recv,
):
    n_tp, n_pp, n_dp, row_blocks = dims
    n_all = n_tp * n_pp * n_dp
    n_half = n_tp // 2
    heads, rows_dev, half_positions, head_dim = cache_buf.shape
    head_dim = head_dim // 2
    tokens, width = product.shape
    steps = tokens // rows_dev
    owners, slots = targets_ref.shape
    piece = width // n_tp
    row_queries = 2 * steps
    group_rows = rows_dev * row_queries
    blocks = group_rows // (16 * PAIRS)
    block_rows = 16 * PAIRS
    slot_rows = 16
    tp = lax.axis_index("tp")
    me = (tp * n_pp + lax.axis_index("pp")) * n_dp + lax.axis_index("dp")
    upper = tp // n_half
    place_in_half = lax.rem(tp, n_half)
    partner = {"tp": lax.rem(tp + n_half, n_tp)}
    scale = 1.0 / math.sqrt(head_dim)
    f32, bf16 = jnp.float32, jnp.bfloat16

    def load(i, source, target):
        copy = pltpu.make_async_copy(source, target, local_sem.at[i])
        copy.start()
        return copy

    small = [
        load(2, scales_hbm, scales_ref),
        load(3, targets_hbm, targets_ref),
        load(4, counts_hbm, counts_ref),
        load(5, values_hbm, values_ref),
    ]
    query_load = load(6, query_hbm, query_raw)
    hidden_load = load(7, hidden_hbm, hidden_ref)
    later = [
        load(8, updated_hbm, updated_ref),
        load(9, lens_hbm, lens_ref),
        load(10, lens_hbm, lens_row),
    ]
    w_copy = load(0, w_hbm, w_buf)

    def cache_copy(g):
        return pltpu.make_async_copy(cache_hbm.at[:, g], cache_buf.at[g], cache_sem.at[g])

    for g in range(heads):
        cache_copy(g).start()

    def place(index):
        return {
            "tp": index // (n_pp * n_dp),
            "pp": lax.rem(index // n_dp, n_pp),
            "dp": lax.rem(index, n_dp),
        }

    barrier = pltpu.get_barrier_semaphore()

    def greet(k, carry):
        pl.semaphore_signal(
            barrier, inc=1, device_id=place(lax.rem(me + k, n_all)), device_id_type=MESH
        )
        return carry

    lax.fori_loop(1, n_all, greet, 0)

    query_load.wait()
    for g in range(heads):
        for t in range(steps):
            for b in range(2):
                lanes = slice((g * 2 + b) * head_dim, (g * 2 + b + 1) * head_dim)
                query_wide[pl.ds(g * group_rows + t * 2 + b, rows_dev, stride=row_queries), :] = (
                    query_raw[t, :, lanes].astype(f32)
                )
    query_ref[...] = query_wide[...].astype(bf16)

    for copy in small:
        copy.wait()
    scales_wide[...] = scales_ref[...].astype(f32)
    row8 = lax.broadcasted_iota(jnp.int32, (slots, slots), 0)
    col8 = lax.broadcasted_iota(jnp.int32, (slots, slots), 1)
    lane = lax.broadcasted_iota(jnp.int32, (slots, 128), 1)
    owner_lane = lax.broadcasted_iota(jnp.int32, counts_ref.shape, 1)

    def pack(o, carry):
        def column(x):
            wide = jnp.where(row8 == col8, jnp.broadcast_to(x, (slots, slots)), 0.0)
            return jnp.sum(wide, -1, keepdims=True)

        count = jnp.sum(jnp.where(owner_lane == o, counts_ref[...].astype(f32), 0.0), -1, keepdims=True)
        scales = scales_wide[pl.ds(o, 1), :]
        scales = jnp.where(col8[:1].astype(f32) < count, scales, 0.0)
        target = targets_ref[pl.ds(o, 1), :]
        shift = row_blocks.bit_length() - 1
        high = (target >> (shift + 4)).astype(f32)
        low = ((target >> shift) & 15).astype(f32)
        block = (target & (row_blocks - 1)).astype(f32)
        meta = jnp.zeros((slots, 128), f32)
        for i, field in enumerate((scales, high, low, block)):
            meta = jnp.where(lane == i, column(field), meta)
        both = jnp.concatenate([values_ref[o].astype(f32), meta], 0)
        packed_ref[pl.ds(pl.multiple_of(o * slot_rows, slot_rows), slot_rows), :] = both.astype(bf16)
        return carry

    lax.fori_loop(0, owners, pack, 0)
    pl.semaphore_wait(barrier, n_all - 1)

    def owner_rows(index):
        return pl.ds(pl.multiple_of((index // n_dp) * slot_rows, slot_rows), slot_rows)

    my_rows = pl.ds(pl.multiple_of(me * slot_rows, slot_rows), slot_rows)

    def delta_copy(k):
        target = lax.rem(me + k, n_all)
        return pltpu.make_async_remote_copy(
            src_ref=packed_ref.at[owner_rows(target)],
            dst_ref=delta_buf.at[my_rows],
            send_sem=delta_send.at[k],
            recv_sem=delta_recv.at[k],
            device_id=place(target),
            device_id_type=MESH,
        )

    def group_slice(g):
        return pl.ds(pl.multiple_of(g * group_rows, group_rows), group_rows)

    def query_copy(g):
        return pltpu.make_async_remote_copy(
            src_ref=query_ref.at[group_slice(g)],
            dst_ref=other_query.at[group_slice(g)],
            send_sem=query_send.at[g],
            recv_sem=query_recv.at[g],
            device_id=partner,
            device_id_type=MESH,
        )

    def back_copy(g):
        return pltpu.make_async_remote_copy(
            src_ref=back_buf.at[group_slice(g)],
            dst_ref=got_buf.at[group_slice(g)],
            send_sem=back_send.at[g],
            recv_sem=back_recv.at[g],
            device_id=partner,
            device_id_type=MESH,
        )

    def start_delta(k, carry):
        delta_copy(k).start()
        return carry

    lax.fori_loop(1, n_all, start_delta, 0)
    own_delta = pltpu.make_async_copy(
        packed_ref.at[owner_rows(me)], delta_buf.at[my_rows], local_sem.at[1]
    )
    own_delta.start()
    for g in range(heads):
        query_copy(g).start()

    hidden_load.wait()
    hidden = hidden_ref[...]
    w_copy.wait()
    tile = 256
    for c in range(width // tile):
        cols = slice(c * tile, (c + 1) * tile)
        product[:, cols] = jnp.dot(hidden, w_buf[:, cols], preferred_element_type=f32)

    for copy in later:
        copy.wait()

    def wait_delta(k, carry):
        delta_copy(k).wait()
        return carry

    lax.fori_loop(1, n_all, wait_delta, 0)
    own_delta.wait()
    shard_rows = hidden.shape[1]
    row_index = lax.broadcasted_iota(jnp.int32, (128, shard_rows), 1).astype(f32)
    taken = jnp.broadcast_to(updated_ref[...], (128, shard_rows)) == 1

    def add_deltas(chunk, carry):
        got = delta_buf[pl.ds(pl.multiple_of(chunk * 256, 256), 256), :].astype(f32)
        got = got.reshape(16, 16, 128)
        values = got[:, :8].reshape(128, 128)
        meta = got[:, 8:].reshape(128, 128)
        row = meta[:, 1:2] * 16.0 + meta[:, 2:3]
        place_row = jnp.where((row_index == row) & taken, meta[:, 0:1], 0.0).astype(bf16)
        picked = lax.dot_general(hidden, place_row, NT, preferred_element_type=f32)
        high = picked.astype(bf16)
        low = (picked - high.astype(f32)).astype(bf16)
        for c in range(width // tile):
            cols = slice(c * tile, (c + 1) * tile)
            spread = jnp.concatenate(
                [
                    jnp.where(meta[:, 3:4] == float(j), values, 0.0)
                    for j in range(c * tile // 128, (c + 1) * tile // 128)
                ],
                1,
            ).astype(bf16)
            product[:, cols] += jnp.dot(high, spread, preferred_element_type=f32) + jnp.dot(
                low, spread, preferred_element_type=f32
            )
        return carry

    lax.fori_loop(0, n_all // 16, add_deltas, 0)
    for j in range(n_half):
        for part in range(2):
            i = part * n_half + j
            send_buf[j, part] = product[:, i * piece : (i + 1) * piece].astype(bf16)

    def sum_copy(k):
        target = lax.rem(place_in_half + k, n_half)
        return pltpu.make_async_remote_copy(
            src_ref=send_buf.at[target],
            dst_ref=sum_buf.at[k],
            send_sem=sum_send.at[k],
            recv_sem=sum_recv.at[k],
            device_id={"tp": upper * n_half + target},
            device_id_type=MESH,
        )

    for k in range(1, n_half):
        sum_copy(k).start()

    def tail_copy(i, source, target):
        return pltpu.make_async_remote_copy(
            src_ref=source,
            dst_ref=target,
            send_sem=tail_send.at[i],
            recv_sem=tail_recv.at[i],
            device_id=partner,
            device_id_type=MESH,
        )

    row16 = lax.broadcasted_iota(jnp.int32, (16, 256), 0)
    col16 = lax.broadcasted_iota(jnp.int32, (16, 256), 1)
    same = (row16 // 8) == (col16 // 128)
    position = lax.rem(col16, 128) + upper * half_positions
    eye = lax.broadcasted_iota(jnp.int32, (128, 128), 0) == lax.broadcasted_iota(
        jnp.int32, (128, 128), 1
    )

    def attend(source, g, block):
        base = block * 2 * PAIRS
        scores, valids = [], []
        start = pl.multiple_of(g * group_rows + block * block_rows, block_rows)
        for i in range(PAIRS):
            r = base + 2 * i
            keys = jnp.concatenate(
                [cache_buf[g, r, :, :head_dim], cache_buf[g, r + 1, :, :head_dim]], 0
            )
            q16 = source[pl.ds(start + 16 * i, 16), :]
            scores.append(lax.dot_general(q16, keys, NT, preferred_element_type=f32))
            length = jnp.where(row16 < 8, lens_ref[r], lens_ref[r + 1])
            valids.append(same & (position < length))
        maxima, totals, outs = [], [], []
        for i in range(PAIRS):
            r = base + 2 * i
            s = jnp.where(valids[i], scores[i] * scale, NEG_FILL)
            m = jnp.max(s, -1, keepdims=True)
            e = jnp.where(valids[i], jnp.exp(s - m), 0.0)
            maxima.append(m)
            totals.append(jnp.sum(e, -1, keepdims=True))
            values = jnp.concatenate(
                [cache_buf[g, r, :, head_dim:], cache_buf[g, r + 1, :, head_dim:]], 0
            )
            outs.append(jnp.dot(e.astype(bf16), values, preferred_element_type=f32))
        return (
            start,
            jnp.concatenate(maxima, 0),
            jnp.concatenate(totals, 0),
            jnp.concatenate(outs, 0),
        )

    def other_group(g, carry):
        cache_copy(g).wait()
        query_copy(g).wait()
        for block in range(blocks):
            start, m, l, o = attend(other_query, g, block)
            back_buf[pl.ds(start, block_rows), :] = o.astype(bf16)
            at = pl.ds(g * blocks + block, 1)
            back_stats[0, at, :] = jnp.sum(jnp.where(eye, m, 0.0), 0, keepdims=True)
            back_stats[1, at, :] = jnp.sum(jnp.where(eye, l, 0.0), 0, keepdims=True)
        back_copy(g).start()
        return carry

    to_column = lax.broadcasted_iota(jnp.int32, (rows_dev, rows_dev), 0) == lax.broadcasted_iota(
        jnp.int32, (rows_dev, rows_dev), 1
    )
    lengths = jnp.broadcast_to(lens_row[...].astype(f32).reshape(1, rows_dev), (rows_dev, rows_dev))
    lengths = jnp.sum(jnp.where(to_column, lengths, 0.0), -1, keepdims=True)
    index = lax.rem(lax.broadcasted_iota(jnp.int32, (1, head_dim), 1), head_dim // 2).astype(f32)
    inverse = jnp.exp(index * (-2.0 / head_dim) * math.log(ROPE_BASE))
    positions = jnp.concatenate([lengths + float(t) for t in range(steps)], 0)
    angles = positions * inverse
    first = lax.broadcasted_iota(jnp.int32, (tokens, head_dim), 1) < head_dim // 2
    sine = jnp.sin(angles)
    cos_ref[...] = jnp.cos(angles)
    sin_ref[...] = jnp.where(first, -sine, sine)

    early = (heads + 1) // 2
    lax.fori_loop(0, early, other_group, 0)

    for k in range(1, n_half):
        sum_copy(k).wait()
    sums = []
    for part in range(2):
        total = send_buf[place_in_half, part].astype(f32)
        for k in range(1, n_half):
            total += sum_buf[k, part].astype(f32)
        sums.append(total)
    kept_sum[...] = jnp.where(upper == 0, sums[0], sums[1])
    pair_buf[...] = jnp.where(upper == 0, sums[1], sums[0]).astype(bf16)
    pair_copy = tail_copy(2, pair_buf, pair_got)
    pair_copy.start()

    lax.fori_loop(early, heads, other_group, 0)
    stats_copy = tail_copy(0, back_stats, got_stats)
    stats_copy.start()

    pair_copy.wait()
    for g in range(heads):
        cols = slice(g * head_dim, (g + 1) * head_dim)
        x = kept_sum[:, cols] + pair_got[:, cols].astype(f32)
        turned = x * cos_ref[...] + pltpu.roll(x, head_dim // 2, 1) * sin_ref[...]
        piece_buf[:, cols] = jnp.where(upper == 0, turned, x).astype(bf16)
    piece_copy = tail_copy(1, piece_buf, other_piece)
    piece_copy.start()
    entries_ref[...] = piece_buf[...]

    def own_group(g, carry):
        for block in range(blocks):
            start, m, l, o = attend(query_ref, g, block)
            where = pl.ds(start, block_rows)
            own_out[where, :] = o
            own_max[where, :] = jnp.broadcast_to(m, (block_rows, 128))
            own_total[where, :] = jnp.broadcast_to(l, (block_rows, 128))
        return carry

    lax.fori_loop(0, heads, own_group, 0)
    piece_copy.wait()

    q_row = lax.broadcasted_iota(jnp.int32, (block_rows, tokens), 0)
    k_col = lax.broadcasted_iota(jnp.int32, (block_rows, tokens), 1)
    step_of = lax.rem(q_row, row_queries) // 2
    seen = k_col // rows_dev <= step_of
    for g in range(heads):
        cols = slice(g * head_dim, (g + 1) * head_dim)
        mine, theirs = piece_buf[:, cols], other_piece[:, cols]
        new_keys = jnp.where(upper == 0, mine, theirs)
        new_values = jnp.where(upper == 0, theirs, mine)
        for block in range(blocks):
            first_row = g * group_rows + block * block_rows
            where = slice(first_row, first_row + block_rows)
            row_of = block * (block_rows // row_queries) + q_row // row_queries
            valid = (row_of == lax.rem(k_col, rows_dev)) & seen
            s = lax.dot_general(query_ref[where, :], new_keys, NT, preferred_element_type=f32)
            s = jnp.where(valid, s * scale, NEG_FILL)
            m1, l1 = own_max[where, :], own_total[where, :]
            top = jnp.maximum(jnp.max(s, -1, keepdims=True), m1)
            e = jnp.where(valid, jnp.exp(s - top), 0.0)
            o3 = jnp.dot(e.astype(bf16), new_values, preferred_element_type=f32)
            f1 = jnp.exp(m1 - top)
            own_out[where, :] = own_out[where, :] * f1 + o3
            own_total[where, :] = l1 * f1 + jnp.sum(e, -1, keepdims=True)
            own_max[where, :] = top

    stats_copy.wait()
    for g in range(heads):
        back_copy(g).wait()
        for block in range(blocks):
            first_row = g * group_rows + block * block_rows
            where = slice(first_row, first_row + block_rows)
            at = g * blocks + block
            m2 = jnp.sum(jnp.where(eye, got_stats[0, at : at + 1, :], 0.0), -1, keepdims=True)
            l2 = jnp.sum(jnp.where(eye, got_stats[1, at : at + 1, :], 0.0), -1, keepdims=True)
            m1 = own_max[where, :]
            top = jnp.maximum(m1, m2)
            f1, f2 = jnp.exp(m1 - top), jnp.exp(m2 - top)
            whole = own_out[where, :] * f1 + got_buf[where, :].astype(f32) * f2
            query_wide[where, :] = whole / (own_total[where, :] * f1 + l2 * f2)
        for t in range(steps):
            for b in range(2):
                lanes = slice((g * 2 + b) * head_dim, (g * 2 + b + 1) * head_dim)
                rows = pl.ds(g * group_rows + t * 2 + b, rows_dev, stride=row_queries)
                out_ref[t, :, lanes] = query_wide[rows, :].astype(bf16)


def shards(
    sizes,
    hidden,
    w_kv,
    queries,
    cache,
    cache_lengths,
    updated,
    delta_values,
    delta_scales,
    delta_targets,
    send_counts,
):
    n_tp, n_pp, n_dp = sizes
    n_all = n_tp * n_pp * n_dp
    owners, slots, block_width = delta_values.shape[1:]
    shard_rows, width = w_kv.shape[1:]
    steps, rows_dev = hidden.shape[1:3]
    heads, half_positions = cache.shape[2:4]
    head_dim = cache.shape[4] // 2
    tokens = steps * rows_dev
    piece = width // n_tp
    all_queries = heads * rows_dev * steps * 2
    bf16, f32, i32 = jnp.bfloat16, jnp.float32, jnp.int32

    vmem = pl.BlockSpec(memory_space=pltpu.VMEM)
    anywhere = pl.BlockSpec(memory_space=pl.ANY)
    stat_rows = max(8, all_queries // 128)
    dma = pltpu.SemaphoreType.DMA
    rows = pltpu.VMEM((all_queries, head_dim), bf16)
    wide_rows = pltpu.VMEM((all_queries, head_dim), f32)
    stats = pltpu.VMEM((2, stat_rows, 128), f32)
    one_piece = pltpu.VMEM((tokens, piece), bf16)
    table = pltpu.VMEM((tokens, head_dim), f32)
    entries, attended = pl.pallas_call(
        functools.partial(kernel, (n_tp, n_pp, n_dp, width // block_width)),
        out_shape=(
            jax.ShapeDtypeStruct((tokens, piece), bf16),
            jax.ShapeDtypeStruct((steps, rows_dev, heads * 2 * head_dim), bf16),
        ),
        in_specs=[anywhere] * 10,
        out_specs=(vmem, vmem),
        scratch_shapes=[
            pltpu.SMEM((rows_dev,), i32),
            pltpu.VMEM((rows_dev,), i32),
            pltpu.VMEM((tokens, shard_rows), bf16),
            pltpu.VMEM((shard_rows, width), bf16),
            pltpu.VMEM((steps, rows_dev, heads * 2 * head_dim), bf16),
            pltpu.VMEM((heads, rows_dev, half_positions, 2 * head_dim), bf16),
            pltpu.VMEM((1, shard_rows), i32),
            pltpu.VMEM((owners, slots, block_width), bf16),
            pltpu.VMEM((owners, slots), bf16),
            pltpu.VMEM((owners, slots), i32),
            pltpu.VMEM((1, owners), i32),
            pltpu.VMEM((owners, slots), f32),
            pltpu.VMEM((owners * 2 * slots, block_width), bf16),
            wide_rows,
            rows,
            table,
            table,
            pltpu.VMEM((n_all * 2 * slots, block_width), bf16),
            pltpu.VMEM((tokens, width), f32),
            pltpu.VMEM((n_tp // 2, 2, tokens, piece), bf16),
            pltpu.VMEM((n_tp // 2, 2, tokens, piece), bf16),
            one_piece,
            one_piece,
            pltpu.VMEM((tokens, piece), f32),
            one_piece,
            one_piece,
            rows,
            rows,
            stats,
            rows,
            stats,
            wide_rows,
            wide_rows,
            wide_rows,
            dma((11,)),
            dma((heads,)),
            dma((n_all,)),
            dma((n_all,)),
            dma((heads,)),
            dma((heads,)),
            dma((n_tp // 2,)),
            dma((n_tp // 2,)),
            dma((heads,)),
            dma((heads,)),
            dma((3,)),
            dma((3,)),
        ],
        compiler_params=pltpu.CompilerParams(
            collective_id=0, has_side_effects=True, vmem_limit_bytes=56 * 1024 * 1024
        ),
        name="decode",
    )(
        cache_lengths,
        hidden[0].reshape(tokens, shard_rows),
        w_kv[0],
        queries[0],
        cache[0],
        updated,
        delta_values[0],
        delta_scales[0],
        delta_targets[0],
        send_counts,
    )
    return (entries.reshape(1, steps, rows_dev, piece), attended[None])


def solution(mesh):
    placed = (
        P(("groups", "pp"), None, "dp", "tp"),
        P(("groups", "pp"), "tp", None),
        P(("groups", "pp"), None, "dp", "tp"),
        P(("groups", "pp"), "dp", "tp", None, None),
        P(("groups", "dp")),
        P(("groups", "pp"), "tp"),
        P(("groups", "tp", "pp", "dp"), None, None, None),
        P(("groups", "tp", "pp", "dp"), None, None),
        P(("groups", "tp", "pp", "dp"), None, None),
        P(("groups", "tp", "pp", "dp"), None),
    )
    sizes = (mesh.shape["tp"], mesh.shape["pp"], mesh.shape["dp"])
    return jax.shard_map(
        functools.partial(shards, sizes),
        mesh=mesh,
        in_specs=placed,
        out_specs=(P(("groups", "pp"), None, "dp", "tp"), P(("groups", "pp"), None, "dp", "tp")),
        check_vma=False,
    )
```

```python
import functools
import math

import jax
import jax.numpy as jnp
from jax import lax
from jax.experimental import pallas as pl
from jax.experimental.pallas import tpu as pltpu
from jax.sharding import PartitionSpec as P

ROPE_BASE = 1000000.0
NEG_FILL = -1e30
MESH = pl.DeviceIdType.MESH
NT = (((1,), (1,)), ((), ()))
PAIRS = 8


def kernel(
    dims,
    lens_hbm,
    hidden_hbm,
    w_hbm,
    query_hbm,
    cache_hbm,
    updated_hbm,
    values_hbm,
    scales_hbm,
    targets_hbm,
    counts_hbm,
    entries_ref,
    out_ref,
    lens_ref,
    lens_row,
    hidden_ref,
    w_buf,
    query_raw,
    cache_buf,
    updated_ref,
    values_ref,
    scales_ref,
    targets_ref,
    counts_ref,
    scales_wide,
    packed_ref,
    query_wide,
    query_ref,
    cos_ref,
    sin_ref,
    delta_buf,
    product,
    send_buf,
    sum_buf,
    pair_buf,
    pair_got,
    kept_sum,
    piece_buf,
    other_piece,
    other_query,
    back_buf,
    back_stats,
    got_buf,
    got_stats,
    own_out,
    own_max,
    own_total,
    local_sem,
    cache_sem,
    delta_send,
    delta_recv,
    query_send,
    query_recv,
    sum_send,
    sum_recv,
    back_send,
    back_recv,
    tail_send,
    tail_recv,
):
    n_tp, n_pp, n_dp, row_blocks = dims
    n_all = n_tp * n_pp * n_dp
    n_half = n_tp // 2
    heads, rows_dev, half_positions, head_dim = cache_buf.shape
    head_dim = head_dim // 2
    tokens, width = product.shape
    steps = tokens // rows_dev
    owners, slots = targets_ref.shape
    piece = width // n_tp
    row_queries = 2 * steps
    group_rows = rows_dev * row_queries
    blocks = group_rows // (16 * PAIRS)
    block_rows = 16 * PAIRS
    slot_rows = 16
    tp = lax.axis_index("tp")
    me = (tp * n_pp + lax.axis_index("pp")) * n_dp + lax.axis_index("dp")
    upper = tp // n_half
    place_in_half = lax.rem(tp, n_half)
    partner = {"tp": lax.rem(tp + n_half, n_tp)}
    scale = 1.0 / math.sqrt(head_dim)
    f32, bf16 = jnp.float32, jnp.bfloat16

    def load(i, source, target):
        copy = pltpu.make_async_copy(source, target, local_sem.at[i])
        copy.start()
        return copy

    small = [
        load(2, scales_hbm, scales_ref),
        load(3, targets_hbm, targets_ref),
        load(4, counts_hbm, counts_ref),
        load(5, values_hbm, values_ref),
    ]
    query_load = load(6, query_hbm, query_raw)
    hidden_load = load(7, hidden_hbm, hidden_ref)
    later = [
        load(8, updated_hbm, updated_ref),
        load(9, lens_hbm, lens_ref),
        load(10, lens_hbm, lens_row),
    ]
    w_copy = load(0, w_hbm, w_buf)

    def cache_copy(g):
        return pltpu.make_async_copy(cache_hbm.at[:, g], cache_buf.at[g], cache_sem.at[g])

    for g in range(heads):
        cache_copy(g).start()

    def place(index):
        return {
            "tp": index // (n_pp * n_dp),
            "pp": lax.rem(index // n_dp, n_pp),
            "dp": lax.rem(index, n_dp),
        }

    barrier = pltpu.get_barrier_semaphore()

    def greet(k, carry):
        pl.semaphore_signal(
            barrier, inc=1, device_id=place(lax.rem(me + k, n_all)), device_id_type=MESH
        )
        return carry

    lax.fori_loop(1, n_all, greet, 0)

    query_load.wait()
    for g in range(heads):
        for t in range(steps):
            for b in range(2):
                lanes = slice((g * 2 + b) * head_dim, (g * 2 + b + 1) * head_dim)
                query_wide[pl.ds(g * group_rows + t * 2 + b, rows_dev, stride=row_queries), :] = (
                    query_raw[t, :, lanes].astype(f32)
                )
    query_ref[...] = query_wide[...].astype(bf16)

    for copy in small:
        copy.wait()
    scales_wide[...] = scales_ref[...].astype(f32)
    row8 = lax.broadcasted_iota(jnp.int32, (slots, slots), 0)
    col8 = lax.broadcasted_iota(jnp.int32, (slots, slots), 1)
    lane = lax.broadcasted_iota(jnp.int32, (slots, 128), 1)
    owner_lane = lax.broadcasted_iota(jnp.int32, counts_ref.shape, 1)

    def pack(o, carry):
        def column(x):
            wide = jnp.where(row8 == col8, jnp.broadcast_to(x, (slots, slots)), 0.0)
            return jnp.sum(wide, -1, keepdims=True)

        count = jnp.sum(jnp.where(owner_lane == o, counts_ref[...].astype(f32), 0.0), -1, keepdims=True)
        scales = scales_wide[pl.ds(o, 1), :]
        scales = jnp.where(col8[:1].astype(f32) < count, scales, 0.0)
        target = targets_ref[pl.ds(o, 1), :]
        shift = row_blocks.bit_length() - 1
        high = (target >> (shift + 4)).astype(f32)
        low = ((target >> shift) & 15).astype(f32)
        block = (target & (row_blocks - 1)).astype(f32)
        meta = jnp.zeros((slots, 128), f32)
        for i, field in enumerate((scales, high, low, block)):
            meta = jnp.where(lane == i, column(field), meta)
        both = jnp.concatenate([values_ref[o].astype(f32), meta], 0)
        packed_ref[pl.ds(pl.multiple_of(o * slot_rows, slot_rows), slot_rows), :] = both.astype(bf16)
        return carry

    lax.fori_loop(0, owners, pack, 0)
    pl.semaphore_wait(barrier, n_all - 1)

    def owner_rows(index):
        return pl.ds(pl.multiple_of((index // n_dp) * slot_rows, slot_rows), slot_rows)

    my_rows = pl.ds(pl.multiple_of(me * slot_rows, slot_rows), slot_rows)

    def delta_copy(k):
        target = lax.rem(me + k, n_all)
        return pltpu.make_async_remote_copy(
            src_ref=packed_ref.at[owner_rows(target)],
            dst_ref=delta_buf.at[my_rows],
            send_sem=delta_send.at[k],
            recv_sem=delta_recv.at[k],
            device_id=place(target),
            device_id_type=MESH,
        )

    def group_slice(g):
        return pl.ds(pl.multiple_of(g * group_rows, group_rows), group_rows)

    def query_copy(g):
        return pltpu.make_async_remote_copy(
            src_ref=query_ref.at[group_slice(g)],
            dst_ref=other_query.at[group_slice(g)],
            send_sem=query_send.at[g],
            recv_sem=query_recv.at[g],
            device_id=partner,
            device_id_type=MESH,
        )

    def back_copy(g):
        return pltpu.make_async_remote_copy(
            src_ref=back_buf.at[group_slice(g)],
            dst_ref=got_buf.at[group_slice(g)],
            send_sem=back_send.at[g],
            recv_sem=back_recv.at[g],
            device_id=partner,
            device_id_type=MESH,
        )

    def start_delta(k, carry):
        delta_copy(k).start()
        return carry

    lax.fori_loop(1, n_all, start_delta, 0)
    own_delta = pltpu.make_async_copy(
        packed_ref.at[owner_rows(me)], delta_buf.at[my_rows], local_sem.at[1]
    )
    own_delta.start()
    early = (heads + 1) // 2
    for g in range(early):
        query_copy(g).start()

    hidden_load.wait()
    hidden = hidden_ref[...]
    w_copy.wait()
    tile = 256
    for c in range(width // tile):
        cols = slice(c * tile, (c + 1) * tile)
        product[:, cols] = jnp.dot(hidden, w_buf[:, cols], preferred_element_type=f32)

    for copy in later:
        copy.wait()

    def wait_delta(k, carry):
        delta_copy(k).wait()
        return carry

    lax.fori_loop(1, n_all, wait_delta, 0)
    own_delta.wait()
    shard_rows = hidden.shape[1]
    row_index = lax.broadcasted_iota(jnp.int32, (128, shard_rows), 1).astype(f32)
    taken = jnp.broadcast_to(updated_ref[...], (128, shard_rows)) == 1

    def add_deltas(chunk, carry):
        got = delta_buf[pl.ds(pl.multiple_of(chunk * 256, 256), 256), :].astype(f32)
        got = got.reshape(16, 16, 128)
        values = got[:, :8].reshape(128, 128)
        meta = got[:, 8:].reshape(128, 128)
        row = meta[:, 1:2] * 16.0 + meta[:, 2:3]
        place_row = jnp.where((row_index == row) & taken, meta[:, 0:1], 0.0).astype(bf16)
        picked = lax.dot_general(hidden, place_row, NT, preferred_element_type=f32)
        high = picked.astype(bf16)
        low = (picked - high.astype(f32)).astype(bf16)
        for c in range(width // tile):
            cols = slice(c * tile, (c + 1) * tile)
            spread = jnp.concatenate(
                [
                    jnp.where(meta[:, 3:4] == float(j), values, 0.0)
                    for j in range(c * tile // 128, (c + 1) * tile // 128)
                ],
                1,
            ).astype(bf16)
            product[:, cols] += jnp.dot(high, spread, preferred_element_type=f32) + jnp.dot(
                low, spread, preferred_element_type=f32
            )
        return carry

    lax.fori_loop(0, n_all // 16, add_deltas, 0)
    for j in range(n_half):
        for part in range(2):
            i = part * n_half + j
            send_buf[j, part] = product[:, i * piece : (i + 1) * piece].astype(bf16)

    def sum_copy(k):
        target = lax.rem(place_in_half + k, n_half)
        return pltpu.make_async_remote_copy(
            src_ref=send_buf.at[target],
            dst_ref=sum_buf.at[k],
            send_sem=sum_send.at[k],
            recv_sem=sum_recv.at[k],
            device_id={"tp": upper * n_half + target},
            device_id_type=MESH,
        )

    for k in range(1, n_half):
        sum_copy(k).start()
    for g in range(early, heads):
        query_copy(g).start()

    def tail_copy(i, source, target):
        return pltpu.make_async_remote_copy(
            src_ref=source,
            dst_ref=target,
            send_sem=tail_send.at[i],
            recv_sem=tail_recv.at[i],
            device_id=partner,
            device_id_type=MESH,
        )

    row16 = lax.broadcasted_iota(jnp.int32, (16, 256), 0)
    col16 = lax.broadcasted_iota(jnp.int32, (16, 256), 1)
    same = (row16 // 8) == (col16 // 128)
    position = lax.rem(col16, 128) + upper * half_positions
    eye = lax.broadcasted_iota(jnp.int32, (128, 128), 0) == lax.broadcasted_iota(
        jnp.int32, (128, 128), 1
    )

    def attend(source, g, block):
        base = block * 2 * PAIRS
        scores, valids = [], []
        start = pl.multiple_of(g * group_rows + block * block_rows, block_rows)
        for i in range(PAIRS):
            r = base + 2 * i
            keys = jnp.concatenate(
                [cache_buf[g, r, :, :head_dim], cache_buf[g, r + 1, :, :head_dim]], 0
            )
            q16 = source[pl.ds(start + 16 * i, 16), :]
            scores.append(lax.dot_general(q16, keys, NT, preferred_element_type=f32))
            length = jnp.where(row16 < 8, lens_ref[r], lens_ref[r + 1])
            valids.append(same & (position < length))
        maxima, totals, outs = [], [], []
        for i in range(PAIRS):
            r = base + 2 * i
            s = jnp.where(valids[i], scores[i] * scale, NEG_FILL)
            m = jnp.max(s, -1, keepdims=True)
            e = jnp.where(valids[i], jnp.exp(s - m), 0.0)
            maxima.append(m)
            totals.append(jnp.sum(e, -1, keepdims=True))
            values = jnp.concatenate(
                [cache_buf[g, r, :, head_dim:], cache_buf[g, r + 1, :, head_dim:]], 0
            )
            outs.append(jnp.dot(e.astype(bf16), values, preferred_element_type=f32))
        return (
            start,
            jnp.concatenate(maxima, 0),
            jnp.concatenate(totals, 0),
            jnp.concatenate(outs, 0),
        )

    def other_group(g, carry):
        cache_copy(g).wait()
        query_copy(g).wait()
        for block in range(blocks):
            start, m, l, o = attend(other_query, g, block)
            back_buf[pl.ds(start, block_rows), :] = o.astype(bf16)
            at = pl.ds(g * blocks + block, 1)
            back_stats[0, at, :] = jnp.sum(jnp.where(eye, m, 0.0), 0, keepdims=True)
            back_stats[1, at, :] = jnp.sum(jnp.where(eye, l, 0.0), 0, keepdims=True)
        return carry

    def other_group_back(g, carry):
        other_group(g, carry)
        back_copy(g).start()
        return carry

    to_column = lax.broadcasted_iota(jnp.int32, (rows_dev, rows_dev), 0) == lax.broadcasted_iota(
        jnp.int32, (rows_dev, rows_dev), 1
    )
    lengths = jnp.broadcast_to(lens_row[...].astype(f32).reshape(1, rows_dev), (rows_dev, rows_dev))
    lengths = jnp.sum(jnp.where(to_column, lengths, 0.0), -1, keepdims=True)
    index = lax.rem(lax.broadcasted_iota(jnp.int32, (1, head_dim), 1), head_dim // 2).astype(f32)
    inverse = jnp.exp(index * (-2.0 / head_dim) * math.log(ROPE_BASE))
    positions = jnp.concatenate([lengths + float(t) for t in range(steps)], 0)
    angles = positions * inverse
    first = lax.broadcasted_iota(jnp.int32, (tokens, head_dim), 1) < head_dim // 2
    sine = jnp.sin(angles)
    cos_ref[...] = jnp.cos(angles)
    sin_ref[...] = jnp.where(first, -sine, sine)

    lax.fori_loop(0, early, other_group, 0)

    for k in range(1, n_half):
        sum_copy(k).wait()
    sums = []
    for part in range(2):
        total = send_buf[place_in_half, part].astype(f32)
        for k in range(1, n_half):
            total += sum_buf[k, part].astype(f32)
        sums.append(total)
    kept_sum[...] = jnp.where(upper == 0, sums[0], sums[1])
    pair_buf[...] = jnp.where(upper == 0, sums[1], sums[0]).astype(bf16)
    pair_copy = tail_copy(2, pair_buf, pair_got)
    pair_copy.start()
    for g in range(early):
        back_copy(g).start()

    lax.fori_loop(early, heads, other_group_back, 0)
    stats_copy = tail_copy(0, back_stats, got_stats)
    stats_copy.start()

    pair_copy.wait()
    for g in range(heads):
        cols = slice(g * head_dim, (g + 1) * head_dim)
        x = kept_sum[:, cols] + pair_got[:, cols].astype(f32)
        turned = x * cos_ref[...] + pltpu.roll(x, head_dim // 2, 1) * sin_ref[...]
        piece_buf[:, cols] = jnp.where(upper == 0, turned, x).astype(bf16)
    piece_copy = tail_copy(1, piece_buf, other_piece)
    piece_copy.start()
    entries_ref[...] = piece_buf[...]

    def own_group(g, carry):
        for block in range(blocks):
            start, m, l, o = attend(query_ref, g, block)
            where = pl.ds(start, block_rows)
            own_out[where, :] = o
            own_max[where, :] = jnp.broadcast_to(m, (block_rows, 128))
            own_total[where, :] = jnp.broadcast_to(l, (block_rows, 128))
        return carry

    lax.fori_loop(0, heads, own_group, 0)
    piece_copy.wait()

    q_row = lax.broadcasted_iota(jnp.int32, (block_rows, tokens), 0)
    k_col = lax.broadcasted_iota(jnp.int32, (block_rows, tokens), 1)
    step_of = lax.rem(q_row, row_queries) // 2
    seen = k_col // rows_dev <= step_of
    for g in range(heads):
        cols = slice(g * head_dim, (g + 1) * head_dim)
        mine, theirs = piece_buf[:, cols], other_piece[:, cols]
        new_keys = jnp.where(upper == 0, mine, theirs)
        new_values = jnp.where(upper == 0, theirs, mine)
        for block in range(blocks):
            first_row = g * group_rows + block * block_rows
            where = slice(first_row, first_row + block_rows)
            row_of = block * (block_rows // row_queries) + q_row // row_queries
            valid = (row_of == lax.rem(k_col, rows_dev)) & seen
            s = lax.dot_general(query_ref[where, :], new_keys, NT, preferred_element_type=f32)
            s = jnp.where(valid, s * scale, NEG_FILL)
            m1, l1 = own_max[where, :], own_total[where, :]
            top = jnp.maximum(jnp.max(s, -1, keepdims=True), m1)
            e = jnp.where(valid, jnp.exp(s - top), 0.0)
            o3 = jnp.dot(e.astype(bf16), new_values, preferred_element_type=f32)
            f1 = jnp.exp(m1 - top)
            own_out[where, :] = own_out[where, :] * f1 + o3
            own_total[where, :] = l1 * f1 + jnp.sum(e, -1, keepdims=True)
            own_max[where, :] = top

    stats_copy.wait()
    for g in range(heads):
        back_copy(g).wait()
        for block in range(blocks):
            first_row = g * group_rows + block * block_rows
            where = slice(first_row, first_row + block_rows)
            at = g * blocks + block
            m2 = jnp.sum(jnp.where(eye, got_stats[0, at : at + 1, :], 0.0), -1, keepdims=True)
            l2 = jnp.sum(jnp.where(eye, got_stats[1, at : at + 1, :], 0.0), -1, keepdims=True)
            m1 = own_max[where, :]
            top = jnp.maximum(m1, m2)
            f1, f2 = jnp.exp(m1 - top), jnp.exp(m2 - top)
            whole = own_out[where, :] * f1 + got_buf[where, :].astype(f32) * f2
            query_wide[where, :] = whole / (own_total[where, :] * f1 + l2 * f2)
        for t in range(steps):
            for b in range(2):
                lanes = slice((g * 2 + b) * head_dim, (g * 2 + b + 1) * head_dim)
                rows = pl.ds(g * group_rows + t * 2 + b, rows_dev, stride=row_queries)
                out_ref[t, :, lanes] = query_wide[rows, :].astype(bf16)


def shards(
    sizes,
    hidden,
    w_kv,
    queries,
    cache,
    cache_lengths,
    updated,
    delta_values,
    delta_scales,
    delta_targets,
    send_counts,
):
    n_tp, n_pp, n_dp = sizes
    n_all = n_tp * n_pp * n_dp
    owners, slots, block_width = delta_values.shape[1:]
    shard_rows, width = w_kv.shape[1:]
    steps, rows_dev = hidden.shape[1:3]
    heads, half_positions = cache.shape[2:4]
    head_dim = cache.shape[4] // 2
    tokens = steps * rows_dev
    piece = width // n_tp
    all_queries = heads * rows_dev * steps * 2
    bf16, f32, i32 = jnp.bfloat16, jnp.float32, jnp.int32

    vmem = pl.BlockSpec(memory_space=pltpu.VMEM)
    anywhere = pl.BlockSpec(memory_space=pl.ANY)
    stat_rows = max(8, all_queries // 128)
    dma = pltpu.SemaphoreType.DMA
    rows = pltpu.VMEM((all_queries, head_dim), bf16)
    wide_rows = pltpu.VMEM((all_queries, head_dim), f32)
    stats = pltpu.VMEM((2, stat_rows, 128), f32)
    one_piece = pltpu.VMEM((tokens, piece), bf16)
    table = pltpu.VMEM((tokens, head_dim), f32)
    entries, attended = pl.pallas_call(
        functools.partial(kernel, (n_tp, n_pp, n_dp, width // block_width)),
        out_shape=(
            jax.ShapeDtypeStruct((tokens, piece), bf16),
            jax.ShapeDtypeStruct((steps, rows_dev, heads * 2 * head_dim), bf16),
        ),
        in_specs=[anywhere] * 10,
        out_specs=(vmem, vmem),
        scratch_shapes=[
            pltpu.SMEM((rows_dev,), i32),
            pltpu.VMEM((rows_dev,), i32),
            pltpu.VMEM((tokens, shard_rows), bf16),
            pltpu.VMEM((shard_rows, width), bf16),
            pltpu.VMEM((steps, rows_dev, heads * 2 * head_dim), bf16),
            pltpu.VMEM((heads, rows_dev, half_positions, 2 * head_dim), bf16),
            pltpu.VMEM((1, shard_rows), i32),
            pltpu.VMEM((owners, slots, block_width), bf16),
            pltpu.VMEM((owners, slots), bf16),
            pltpu.VMEM((owners, slots), i32),
            pltpu.VMEM((1, owners), i32),
            pltpu.VMEM((owners, slots), f32),
            pltpu.VMEM((owners * 2 * slots, block_width), bf16),
            wide_rows,
            rows,
            table,
            table,
            pltpu.VMEM((n_all * 2 * slots, block_width), bf16),
            pltpu.VMEM((tokens, width), f32),
            pltpu.VMEM((n_tp // 2, 2, tokens, piece), bf16),
            pltpu.VMEM((n_tp // 2, 2, tokens, piece), bf16),
            one_piece,
            one_piece,
            pltpu.VMEM((tokens, piece), f32),
            one_piece,
            one_piece,
            rows,
            rows,
            stats,
            rows,
            stats,
            wide_rows,
            wide_rows,
            wide_rows,
            dma((11,)),
            dma((heads,)),
            dma((n_all,)),
            dma((n_all,)),
            dma((heads,)),
            dma((heads,)),
            dma((n_tp // 2,)),
            dma((n_tp // 2,)),
            dma((heads,)),
            dma((heads,)),
            dma((3,)),
            dma((3,)),
        ],
        compiler_params=pltpu.CompilerParams(
            collective_id=0, has_side_effects=True, vmem_limit_bytes=56 * 1024 * 1024
        ),
        name="decode",
    )(
        cache_lengths,
        hidden[0].reshape(tokens, shard_rows),
        w_kv[0],
        queries[0],
        cache[0],
        updated,
        delta_values[0],
        delta_scales[0],
        delta_targets[0],
        send_counts,
    )
    return (entries.reshape(1, steps, rows_dev, piece), attended[None])


def solution(mesh):
    placed = (
        P(("groups", "pp"), None, "dp", "tp"),
        P(("groups", "pp"), "tp", None),
        P(("groups", "pp"), None, "dp", "tp"),
        P(("groups", "pp"), "dp", "tp", None, None),
        P(("groups", "dp")),
        P(("groups", "pp"), "tp"),
        P(("groups", "tp", "pp", "dp"), None, None, None),
        P(("groups", "tp", "pp", "dp"), None, None),
        P(("groups", "tp", "pp", "dp"), None, None),
        P(("groups", "tp", "pp", "dp"), None),
    )
    sizes = (mesh.shape["tp"], mesh.shape["pp"], mesh.shape["dp"])
    return jax.shard_map(
        functools.partial(shards, sizes),
        mesh=mesh,
        in_specs=placed,
        out_specs=(P(("groups", "pp"), None, "dp", "tp"), P(("groups", "pp"), None, "dp", "tp")),
        check_vma=False,
    )
```
